32 devices in a mesh: leaf: 16 (over z, x, core), rhs: 2 (over y).
Axes of the slice: x: 2, y: 2, z: 4, core: 2. Of those that a mesh axis runs over, the one named last changes fastest.
Arguments:
- vectors: bfloat16 [64, 65536], P('rhs', 'leaf'), may hold values from -6 to 6
- leaf_basis: bfloat16 [1024, 64, 64], P('leaf'), may hold values from -0.75 to 0.75
- local_transfer: bfloat16 [2032, 64, 64], P('leaf'), may hold values from -0.5 to 0.5
- coupling: bfloat16 [2032, 4, 64, 64], P('leaf'), may hold values from -0.375 to 0.375
- coupling_source: int32 [2032, 4], P('leaf'), may hold values from 0 to 1023, as said below
- top_transfer: bfloat16 [14, 64, 64], replicated, may hold values from -0.5 to 0.5
- top_coupling: bfloat16 [64, 64, 64], P('leaf'), may hold values from -0.75 to 0.75
- top_target: int32 [64], P('leaf'), may hold values from 2 to 15, as said below
- top_source: int32 [64], P('leaf'), may hold values from 2 to 15, as said below
- near_blocks: bfloat16 [1024, 8, 64, 64], P('leaf', 'rhs'), may hold values from -0.25 to 0.25
- near_source: int32 [1024, 8], P('leaf', 'rhs'), may hold values from 0 to 1023, as said below
Outputs:
- product: bfloat16 [64, 65536], P('rhs', 'leaf')
The draws below stay inside these ranges and needn't reach their ends.
Inputs may be any that keep to these rules, and one draw needn't show every extreme that they name: `coupling_source`: entry k of a row names a node of that row's level other than the row's own node, at most n away from it along the level, where n is the level's nodes of one subtree; entry 0 is the node's sibling. near_source[t, 0] is t; every other entry of row t lies within 64 leaves of t and differs from t. `top_target`: an upper heap node; top_target[b] and top_source[b] are different nodes of the same upper level. `top_source`: an upper heap node of the same level as top_target[b], never equal to it.
All inputs are finite; a program needn't handle non-finite values.
Results may differ from the reference program's by a relative error of at most 0.025.
Values may be sent and summed in bfloat16 or wider, within the bound.
A program may use at most 128 MiB of HBM per device.

```python
import jax
import jax.numpy as jnp
import numpy as np
from jax import lax

LEAF = 64
RANK = 64
RHS = 64
K = 4
NEAR = 8
K_TOP = 4
LEAF_DEV = 64
LEAVES = 1024
POINTS = 65536
NODES_DEV = 127
N_LEAF = 16


def reflect_offsets(key, target, reach, limit, slots):
    key_size, key_sign = jax.random.split(key)
    magnitude = jax.random.randint(key_size, (target.shape[0], slots), 0, 1 << 20) % reach[:, None] + 1
    upward = jax.random.randint(key_sign, (target.shape[0], slots), 0, 2)
    offset = jnp.where(upward == 1, magnitude, -magnitude)
    candidate = target[:, None] + offset
    inside = (candidate >= 0) & (candidate < limit[:, None])
    return jnp.where(inside, candidate, target[:, None] - offset).astype(jnp.int32)


def draw_coupling_source(key, part):
    key = jax.random.fold_in(key, 11)
    node_total = 2 * LEAF_DEV - 1
    per_level = []
    position = []
    node_count = LEAF_DEV
    while node_count >= 1:
        per_level.append(np.full(node_count, node_count))
        position.append(np.arange(node_count))
        node_count //= 2
    per_level = np.concatenate(per_level)
    position = np.concatenate(position)
    row_ids = np.arange(N_LEAF * node_total)
    per_row = per_level[row_ids % node_total]
    target_np = row_ids // node_total * per_row + position[row_ids % node_total]
    target = jnp.asarray(target_np, jnp.int32)
    reach = jnp.asarray(per_row, jnp.int32)
    limit = jnp.asarray(per_row * N_LEAF, jnp.int32)
    chosen = reflect_offsets(key, target, reach, limit, K)
    sibling = jnp.where(target % 2 == 0, target + 1, target - 1)
    return chosen.at[:, 0].set(sibling)


def draw_near_source(key, part):
    key = jax.random.fold_in(key, 12)
    target = jnp.arange(LEAVES, dtype=jnp.int32)
    reach = jnp.full((LEAVES,), LEAF_DEV, jnp.int32)
    limit = jnp.full((LEAVES,), LEAVES, jnp.int32)
    chosen = reflect_offsets(key, target, reach, limit, NEAR)
    return chosen.at[:, 0].set(target)


def upper_pairs(key):
    block_total = N_LEAF * K_TOP
    key_target, key_offset = jax.random.split(jax.random.fold_in(key, 21))
    target = jax.random.randint(key_target, (block_total,), 2, N_LEAF)
    lowest = jnp.full((block_total,), 2, jnp.int32)
    power = 4
    while power < N_LEAF:
        lowest = jnp.where(target >= power, power, lowest)
        power *= 2
    offset = jax.random.randint(key_offset, (block_total,), 0, 1 << 20) % (lowest - 1) + 1
    source = lowest + (target - lowest + offset) % lowest
    target = target.at[0].set(2).at[1].set(N_LEAF - 1)
    source = source.at[0].set(3).at[1].set(N_LEAF - 2)
    return (target.astype(jnp.int32), source.astype(jnp.int32))


def draw_top_target(key, part):
    chosen = upper_pairs(key)
    return chosen[0]


def draw_top_source(key, part):
    chosen = upper_pairs(key)
    return chosen[1]


def steps_of(rng, dims, cuts, low, high):
    factor_of, own = 1.0, jax.random.fold_in(rng, 6)
    for dim, parts in cuts:
        heights = jnp.exp(jax.random.uniform(jax.random.fold_in(own, dim), (parts,), jnp.float32, low / len(cuts), high / len(cuts)))
        factor_of = factor_of * jnp.repeat(heights, dims[dim] // parts).reshape([-1 if axis == dim else 1 for axis in range(len(dims))])
    return factor_of


def bell_draw(rng, extent, width, most, cuts=(), kind=jnp.bfloat16):
    level = steps_of(rng, extent, cuts, -0.22, 0.18) if cuts else 1.0
    result = jax.random.normal(rng, extent, jnp.float32) * width * level
    return jnp.minimum(jnp.maximum(result, -most), most).astype(kind)


def setup_inputs(seed: int = 0) -> dict:
    seeds = jax.random.split(jax.random.key(seed), 12)
    vectors = bell_draw(seeds[0], (RHS, POINTS), 1.0, 6.0, ((0, 2), (1, 16)))
    leaf_basis = bell_draw(seeds[1], (LEAVES, LEAF, RANK), LEAF ** -0.5, 0.75, ((0, 16),))
    local_transfer = bell_draw(seeds[2], (N_LEAF * NODES_DEV, RANK, RANK), (2 * RANK) ** -0.5, 0.5, ((0, 16),))
    coupling = bell_draw(seeds[3], (N_LEAF * NODES_DEV, K, RANK, RANK), (K * RANK) ** -0.5, 0.375, ((0, 16),))
    coupling_source = draw_coupling_source(jax.random.fold_in(seeds[11], 71), 0)
    top_transfer = bell_draw(seeds[5], (N_LEAF - 2, RANK, RANK), (2 * RANK) ** -0.5, 0.5)
    top_coupling = bell_draw(seeds[6], (N_LEAF * K_TOP, RANK, RANK), RANK ** -0.5, 0.75, ((0, 16),))
    top_target = draw_top_target(jax.random.fold_in(seeds[11], 71), 0)
    top_source = draw_top_source(jax.random.fold_in(seeds[11], 71), 0)
    near_blocks = bell_draw(seeds[9], (LEAVES, NEAR, LEAF, LEAF), (NEAR * LEAF) ** -0.5, 0.25, ((0, 16), (1, 2)))
    near_source = draw_near_source(jax.random.fold_in(seeds[11], 71), 0)
    return {"vectors": vectors, "leaf_basis": leaf_basis, "local_transfer": local_transfer, "coupling": coupling, "coupling_source": coupling_source, "top_transfer": top_transfer, "top_coupling": top_coupling, "top_target": top_target, "top_source": top_source, "near_blocks": near_blocks, "near_source": near_source}


full_precision = lax.Precision.HIGHEST


def level_table(leaf_count):
    layout = []
    first_node = 0
    node_count = leaf_count
    while node_count >= 1:
        layout.append((first_node, node_count))
        first_node += node_count
        node_count //= 2
    return layout


def level_rows(stacked, first_node, node_count):
    picked = stacked[:, first_node:first_node + node_count]
    return picked.reshape((stacked.shape[0] * node_count,) + picked.shape[2:])


def descend(upper_field, top_transfer, root_count):
    upper_down = upper_field[:, 2:4]
    level_size = 4
    while level_size < root_count:
        parents = jnp.repeat(upper_down, 2, axis=1)
        transfer_rows = top_transfer[level_size - 2:2 * level_size - 2].astype(jnp.float32)
        upper_down = upper_field[:, level_size:2 * level_size] + jnp.einsum('rhb,hab->rha', parents, transfer_rows, precision=full_precision)
        level_size *= 2
    return upper_down


def reference(vectors, leaf_basis, local_transfer, coupling, coupling_source, top_transfer, top_coupling, top_target, top_source, near_blocks, near_source):
    layout = level_table(LEAF_DEV)
    node_total = 2 * LEAF_DEV - 1
    leaf_points = vectors.reshape(RHS, LEAVES, LEAF)
    transfer = local_transfer.reshape(N_LEAF, node_total, RANK, RANK)
    blocks = coupling.reshape(N_LEAF, node_total, K, RANK, RANK)
    sources = coupling_source.reshape(N_LEAF, node_total, K)
    coefficients = [jnp.einsum('rip,ipk->rik', leaf_points.astype(jnp.float32), leaf_basis.astype(jnp.float32), precision=full_precision).astype(jnp.bfloat16)]
    for height in range(1, len(layout)):
        first_node, node_count = layout[height - 1]
        transfer_rows = level_rows(transfer, first_node, node_count).astype(jnp.float32)
        lifted = jnp.einsum('rik,ikm->rim', coefficients[-1].astype(jnp.float32), transfer_rows, precision=full_precision)
        coefficients.append(lifted.reshape(RHS, -1, 2, RANK).sum(axis=2).astype(jnp.bfloat16))
    fields = []
    for height in range(len(layout)):
        first_node, node_count = layout[height]
        level_blocks = level_rows(blocks, first_node, node_count)
        level_sources = level_rows(sources, first_node, node_count)
        summed = jnp.zeros((RHS, N_LEAF * node_count, RANK), jnp.float32)
        for slot in range(K):
            picked = jnp.take(coefficients[height], level_sources[:, slot], axis=1).astype(jnp.float32)
            summed = summed + jnp.einsum('rtm,tmn->rtn', picked, level_blocks[:, slot].astype(jnp.float32), precision=full_precision)
        fields.append(summed)
    root_transfer = transfer[:, node_total - 1].astype(jnp.float32)
    root_term = jnp.einsum('rdk,dkm->rdm', coefficients[-1].astype(jnp.float32), root_transfer, precision=full_precision)
    upper = [root_term.reshape(RHS, N_LEAF // 2, 2, RANK).sum(axis=2).astype(jnp.bfloat16)]
    level_size = N_LEAF // 2
    while level_size > 2:
        transfer_rows = top_transfer[level_size - 2:2 * level_size - 2].astype(jnp.float32)
        lifted = jnp.einsum('rhk,hkm->rhm', upper[0].astype(jnp.float32), transfer_rows, precision=full_precision)
        upper.insert(0, lifted.reshape(RHS, level_size // 2, 2, RANK).sum(axis=2).astype(jnp.bfloat16))
        level_size //= 2
    heap_coef = jnp.concatenate([jnp.zeros((RHS, 2, RANK), jnp.bfloat16)] + upper, axis=1)
    picked = jnp.take(heap_coef, top_source, axis=1).astype(jnp.float32)
    contrib = jnp.einsum('rbm,bmn->rbn', picked, top_coupling.astype(jnp.float32), precision=full_precision)
    upper_field = jnp.zeros((RHS, N_LEAF, RANK), jnp.float32).at[:, top_target].add(contrib)
    upper_down = descend(upper_field, top_transfer, N_LEAF)
    parents = jnp.repeat(upper_down, 2, axis=1)
    descent = (fields[-1] + jnp.einsum('rdb,dab->rda', parents, root_transfer, precision=full_precision)).astype(jnp.bfloat16)
    for height in range(len(layout) - 2, -1, -1):
        first_node, node_count = layout[height]
        transfer_rows = level_rows(transfer, first_node, node_count).astype(jnp.float32)
        parents = jnp.repeat(descent, 2, axis=1).astype(jnp.float32)
        descent = (fields[height] + jnp.einsum('rtb,tab->rta', parents, transfer_rows, precision=full_precision)).astype(jnp.bfloat16)
    far_part = jnp.einsum('rik,ipk->rip', descent.astype(jnp.float32), leaf_basis.astype(jnp.float32), precision=full_precision)
    near_sum = jnp.zeros((RHS, LEAVES, LEAF), jnp.float32)
    for slot in range(NEAR):
        picked = jnp.take(leaf_points, near_source[:, slot], axis=1).astype(jnp.float32)
        near_sum = near_sum + jnp.einsum('riq,ipq->rip', picked, near_blocks[:, slot].astype(jnp.float32), precision=full_precision)
    return (far_part + near_sum).reshape(RHS, POINTS).astype(jnp.bfloat16)
```

```python
import functools

import jax
import jax.numpy as jnp
from jax import lax
from jax.experimental import pallas as pl
from jax.experimental.pallas import tpu as pltpu
from jax.sharding import PartitionSpec as P

MESH = pl.DeviceIdType.MESH
NT = (((1,), (1,)), ((), ()))
NN = (((1,), (0,)), ((), ()))
f32 = jnp.float32
bf16 = jnp.bfloat16


def mm(a, b, dims=NN):
    return lax.dot_general(a, b, dims, preferred_element_type=f32)


def mm_split(a, b, dims):
    high = a.astype(bf16)
    low = (a - high.astype(f32)).astype(bf16)
    return mm(high, b, dims) + mm(low, b, dims)


def level_table(leaf_count):
    layout = []
    first, count, pair = 0, leaf_count, 0
    while count >= 1:
        layout.append((first, count, pair))
        first += count
        pair += max(count // 2, 1)
        count //= 2
    return layout


def loop(count, body, unroll):
    unroll = min(unroll, count)
    while count % unroll:
        unroll -= 1

    def step(i, carry):
        for u in range(unroll):
            body(i * unroll + u)
        return carry

    if count == unroll:
        step(0, 0)
    else:
        lax.fori_loop(0, count // unroll, step, 0)


def kernel(
    roots_n,
    vec, basis_h, trans_h, coup_h, near_h,
    cs, ns, tt, ts, top_t, top_c,
    out,
    vbuf, pts, basis, trans, coup, near,
    cp, halo, cl, field, down, near_own, near_send, near_recv,
    roots, uc, g, top_recv,
    local_sem, vs_sem, vr_sem, hs_sem, hr_sem, ns_sem, nr_sem, rs_sem, rr_sem, ts_sem, tr_sem,
):
    n = roots_n
    leaves = basis.shape[0]
    width = basis.shape[1]
    rows = vec.shape[0]
    layout = level_table(leaves)
    pairs = leaves // 2
    slots = coup.shape[1]
    near_slots = near.shape[1]
    top_blocks = top_c.shape[0]
    me = lax.axis_index("leaf")
    mine = lax.axis_index("rhs")
    other = 1 - mine
    has_left, has_right = me > 0, me < n - 1

    def peer_of(i):
        return lax.rem(me + i, n)

    barrier = pltpu.get_barrier_semaphore()

    def greet(i, carry):
        pl.semaphore_signal(barrier, inc=1, device_id=(peer_of(i), mine), device_id_type=MESH)
        return carry

    lax.fori_loop(1, n, greet, 0)
    pl.semaphore_signal(barrier, inc=1, device_id=(me, other), device_id_type=MESH)

    @pl.when(has_left)
    def _():
        pl.semaphore_signal(barrier, inc=1, device_id=(me - 1, other), device_id_type=MESH)

    @pl.when(has_right)
    def _():
        pl.semaphore_signal(barrier, inc=1, device_id=(me + 1, other), device_id_type=MESH)

    local = [
        pltpu.make_async_copy(src, dst, local_sem.at[i])
        for i, (src, dst) in enumerate(
            ((vec, vbuf.at[1, 0]), (basis_h, basis), (trans_h, trans), (near_h, near), (coup_h, coup))
        )
    ]
    for copy in local:
        copy.start()

    pl.semaphore_wait(barrier, n + jnp.where(has_left, 1, 0) + jnp.where(has_right, 1, 0))

    def vec_send(place, half):
        target = (me + (1 - place), mine if half == 0 else other)
        return pltpu.make_async_remote_copy(
            src_ref=vec, dst_ref=vbuf.at[place, half],
            send_sem=vs_sem.at[place, half], recv_sem=vr_sem.at[place, half],
            device_id=target, device_id_type=MESH,
        )

    def halo_send(place, part):
        part_pairs = pl.ds(0, pairs) if part == 0 else pl.ds(pairs, cp.shape[0] - pairs)
        return pltpu.make_async_remote_copy(
            src_ref=cp.at[part_pairs], dst_ref=halo.at[place, part_pairs],
            send_sem=hs_sem.at[place, part], recv_sem=hr_sem.at[place, part],
            device_id=(me + (1 - 2 * place), mine), device_id_type=MESH,
        )

    sends_right, sends_left = has_right, has_left
    vec_send(1, 1).start()

    @pl.when(sends_right)
    def _():
        vec_send(0, 0).start()
        vec_send(0, 1).start()

    @pl.when(sends_left)
    def _():
        vec_send(2, 0).start()
        vec_send(2, 1).start()

    local[0].wait()
    local[1].wait()

    def store_pair(pair_index, node_index, a, b):
        cp[pair_index] = jnp.concatenate([a, b], axis=1)
        cl[node_index] = a
        cl[node_index + 1] = b

    def leaf_up(p):
        x = vbuf[1, 0, :, pl.ds(pl.multiple_of(p * 2 * width, 2 * width), 2 * width)]
        x0, x1 = x[:, :width], x[:, width:]
        c0 = mm(x0, basis[2 * p]).astype(bf16)
        c1 = mm(x1, basis[2 * p + 1]).astype(bf16)
        store_pair(p, leaves + 2 * p, c0, c1)

    loop(pairs, leaf_up, 4)

    @pl.when(sends_right)
    def _():
        halo_send(0, 0).start()

    @pl.when(sends_left)
    def _():
        halo_send(1, 0).start()

    local[2].wait()
    for height in range(1, len(layout)):
        below_first, below_count, below_pair = layout[height - 1]
        first, count, pair = layout[height]

        def lift(q):
            w = trans[pl.ds(below_first + 2 * q, 2)].reshape(2 * width, width)
            return mm(cp[below_pair + q], w).astype(bf16)

        if count > 1:
            def up(p):
                store_pair(pair + p, 3 * first + count + 2 * p, lift(2 * p), lift(2 * p + 1))

            loop(count // 2, up, 4)
        else:
            c = lift(0)
            cp[pair] = jnp.concatenate([c, c], axis=1)
            cl[3 * first + count] = c
    root_row = layout[-1][0]
    root_pair = layout[-1][2]
    root_term = mm(cp[root_pair][:, :width], trans[root_row])
    roots[me] = root_term

    def root_copy(i):
        return pltpu.make_async_remote_copy(
            src_ref=roots.at[me], dst_ref=roots.at[me],
            send_sem=rs_sem.at[i], recv_sem=rr_sem.at[me],
            device_id=(peer_of(i), mine), device_id_type=MESH,
        )

    def root_recv(i):
        source = peer_of(i)
        return pltpu.make_async_remote_copy(
            src_ref=roots.at[source], dst_ref=roots.at[source],
            send_sem=rs_sem.at[i], recv_sem=rr_sem.at[source],
            device_id=(source, mine), device_id_type=MESH,
        )

    def send_roots(i, carry):
        root_copy(i).start()
        return carry

    lax.fori_loop(1, n, send_roots, 0)

    @pl.when(sends_right)
    def _():
        halo_send(0, 1).start()

    @pl.when(sends_left)
    def _():
        halo_send(1, 1).start()

    def unpack_points(place, half):
        def body(p):
            x = vbuf[place, half, :, pl.ds(pl.multiple_of(p * 2 * width, 2 * width), 2 * width)]
            pts[place * leaves + 2 * p, half * rows:(half + 1) * rows, :] = x[:, :width]
            pts[place * leaves + 2 * p + 1, half * rows:(half + 1) * rows, :] = x[:, width:]

        loop(pairs, body, 8)

    unpack_points(1, 0)

    @pl.when(jnp.logical_not(has_left))
    def _():
        vbuf[0] = jnp.zeros(vbuf.shape[1:], bf16)
        halo[0] = jnp.zeros(halo.shape[1:], bf16)

    @pl.when(jnp.logical_not(has_right))
    def _():
        vbuf[2] = jnp.zeros(vbuf.shape[1:], bf16)
        halo[1] = jnp.zeros(halo.shape[1:], bf16)

    vec_send(1, 1).wait_recv()
    unpack_points(1, 1)
    for half in range(2):
        @pl.when(has_left)
        def _():
            vec_send(0, half).wait_recv()

        unpack_points(0, half)

        @pl.when(has_right)
        def _():
            vec_send(2, half).wait_recv()

        unpack_points(2, half)

    local[3].wait()
    leaf_base = (me - 1) * leaves

    def near_leaf(i):
        total = None
        for j in range(near_slots):
            term = mm(pts[jnp.clip(ns[j, i] - leaf_base, 0, 3 * leaves - 1)], near[i, j], NT)
            total = term if total is None else total + term
        return total

    def near_pair(p):
        both = jnp.concatenate([near_leaf(2 * p), near_leaf(2 * p + 1)], axis=1)
        near_own[p] = both[:rows]
        near_send[p] = both[rows:].astype(bf16)

    chunks = near_recv_chunks = ns_sem.shape[0]
    chunk = pairs // chunks

    def near_copy(c):
        part = pl.ds(c * chunk, chunk)
        return pltpu.make_async_remote_copy(
            src_ref=near_send.at[part], dst_ref=near_recv.at[part],
            send_sem=ns_sem.at[c], recv_sem=nr_sem.at[c],
            device_id=(me, other), device_id_type=MESH,
        )

    for c in range(chunks):
        loop(chunk, lambda p: near_pair(c * chunk + p), 2)
        near_copy(c).start()

    def recv_roots(i, carry):
        root_recv(i).wait_recv()
        return carry

    lax.fori_loop(1, n, recv_roots, 0)
    half_n = n // 2
    uc[0] = jnp.zeros(uc.shape[1:], bf16)
    uc[1] = jnp.zeros(uc.shape[1:], bf16)
    loop(half_n, lambda j: uc.__setitem__(half_n + j, (roots[2 * j] + roots[2 * j + 1]).astype(bf16)), 4)
    size = half_n // 2
    while size >= 2:
        def upper_up(j):
            h = size + j
            x = mm(uc[2 * h], top_t[2 * h - 2]) + mm(uc[2 * h + 1], top_t[2 * h - 1])
            uc[h] = x.astype(bf16)

        loop(size, upper_up, 4)
        size //= 2
    terms = [mm(uc[ts[b]], top_c[b]) for b in range(top_blocks)]

    def upper_gather(j):
        h = j + 2
        total = None
        for b in range(top_blocks):
            term = terms[b] * (tt[b] == h).astype(f32)
            total = term if total is None else total + term
        g[h] = total

    loop(n - 2, upper_gather, 2)
    size = 2
    while size < half_n:
        def upper_down(j):
            h = size + j
            w = top_t[pl.ds(2 * h - 2, 2)].reshape(2 * width, width)
            x = mm_split(g[h], w, NT)
            g[2 * h] = g[2 * h] + x[:, :width]
            g[2 * h + 1] = g[2 * h + 1] + x[:, width:]

        loop(size, upper_down, 4)
        size *= 2

    def top_copy(i):
        peer = peer_of(i)
        return pltpu.make_async_remote_copy(
            src_ref=g.at[half_n + peer // 2], dst_ref=top_recv.at[me],
            send_sem=ts_sem.at[i], recv_sem=tr_sem.at[me],
            device_id=(peer, mine), device_id_type=MESH,
        )

    def top_wait(i):
        source = peer_of(i)
        return pltpu.make_async_remote_copy(
            src_ref=g.at[half_n + source // 2], dst_ref=top_recv.at[source],
            send_sem=ts_sem.at[i], recv_sem=tr_sem.at[source],
            device_id=(source, mine), device_id_type=MESH,
        )

    def send_top(i, carry):
        top_copy(i).start()
        return carry

    lax.fori_loop(1, n, send_top, 0)

    for part in range(2):
        @pl.when(has_left)
        def _():
            halo_send(0, part).wait_recv()

        @pl.when(has_right)
        def _():
            halo_send(1, part).wait_recv()

    for first, count, pair in layout:
        for place in range(2):
            base = 3 * first + 2 * place * count
            if count > 1:
                def unpack(p):
                    x = halo[place, pair + p]
                    cl[base + 2 * p] = x[:, :width]
                    cl[base + 2 * p + 1] = x[:, width:]

                loop(count // 2, unpack, 8)
            else:
                cl[base] = halo[place, pair][:, :width]

    local[4].wait()
    for first, count, pair in layout:
        base = 3 * first - (me - 1) * count

        def node_field(t):
            sources = [jnp.clip(base + cs[k, first + t], 0, cl.shape[0] - 1) for k in range(slots)]
            x = jnp.concatenate([cl[source] for source in sources], axis=1)
            return mm(x, coup[first + t].reshape(slots * width, width))

        if count > 1:
            def pair_field(p):
                field[pair + p] = jnp.concatenate([node_field(2 * p), node_field(2 * p + 1)], axis=1)

            loop(count // 2, pair_field, 4)
        else:
            root_field = node_field(0)

    def recv_top(i, total):
        top_wait(i).wait_recv()
        return total + top_recv[peer_of(i)]

    parent = lax.fori_loop(1, n, recv_top, g[half_n + me // 2])
    root_down = (root_field + mm_split(parent, trans[root_row], NT)).astype(bf16)

    def step_down(height, q, x):
        first, count, pair = layout[height]
        w = trans[pl.ds(first + 2 * q, 2)].reshape(2 * width, width)
        return (field[pair + q] + mm(x, w, NT)).astype(bf16)

    top_height = len(layout) - 2
    down[layout[top_height][2]] = step_down(top_height, 0, root_down)
    for height in range(top_height - 1, 0, -1):
        pair = layout[height][2]
        above = layout[height + 1][2]

        def descend(p):
            x = down[above + p]
            down[pair + 2 * p] = step_down(height, 2 * p, x[:, :width])
            down[pair + 2 * p + 1] = step_down(height, 2 * p + 1, x[:, width:])

        loop(layout[height][1] // 4, descend, 4)

    for c in range(chunks):
        near_copy(c).wait_recv()
    above = layout[1][2]

    def leaf_pair(p, x):
        y = step_down(0, p, x)
        far = jnp.concatenate(
            [mm(y[:, :width], basis[2 * p], NT), mm(y[:, width:], basis[2 * p + 1], NT)], axis=1
        )
        total = far + (near_own[p] + near_recv[p].astype(f32))
        out[:, pl.ds(pl.multiple_of(p * 2 * width, 2 * width), 2 * width)] = total.astype(bf16)

    def leaf_down(p):
        x = down[above + p]
        leaf_pair(2 * p, x[:, :width])
        leaf_pair(2 * p + 1, x[:, width:])

    loop(pairs // 2, leaf_down, 2)

    vec_send(1, 1).wait_send()

    @pl.when(sends_right)
    def _():
        for part in range(2):
            vec_send(0, part).wait_send()
            halo_send(0, part).wait_send()

    @pl.when(sends_left)
    def _():
        for part in range(2):
            vec_send(2, part).wait_send()
            halo_send(1, part).wait_send()

    for c in range(chunks):
        near_copy(c).wait_send()

    def end_sends(i, carry):
        root_copy(i).wait_send()
        top_copy(i).wait_send()
        return carry

    lax.fori_loop(1, n, end_sends, 0)


def shards(
    vectors, leaf_basis, local_transfer, coupling, coupling_source,
    top_transfer, top_coupling, top_target, top_source, near_blocks, near_source,
):
    n = lax.axis_size("leaf")
    rows = vectors.shape[0]
    leaves, width, rank = leaf_basis.shape
    nodes = local_transfer.shape[0]
    pairs = leaves // 2
    pair_total = leaves
    chunks = 4
    any_spec = pl.BlockSpec(memory_space=pl.ANY)
    smem = pl.BlockSpec(memory_space=pltpu.SMEM)
    vmem = pl.BlockSpec(memory_space=pltpu.VMEM)
    dma = pltpu.SemaphoreType.DMA
    return pl.pallas_call(
        functools.partial(kernel, n),
        out_shape=jax.ShapeDtypeStruct(vectors.shape, bf16),
        in_specs=[any_spec] * 5 + [smem] * 4 + [vmem] * 2,
        out_specs=vmem,
        scratch_shapes=[
            pltpu.VMEM((3, 2) + vectors.shape, bf16),
            pltpu.VMEM((3 * leaves, 2 * rows, width), bf16),
            pltpu.VMEM(leaf_basis.shape, bf16),
            pltpu.VMEM(local_transfer.shape, bf16),
            pltpu.VMEM(coupling.shape, bf16),
            pltpu.VMEM(near_blocks.shape, bf16),
            pltpu.VMEM((pair_total, rows, 2 * rank), bf16),
            pltpu.VMEM((2, pair_total, rows, 2 * rank), bf16),
            pltpu.VMEM((3 * nodes, rows, rank), bf16),
            pltpu.VMEM((pair_total, rows, 2 * rank), f32),
            pltpu.VMEM((pair_total, rows, 2 * rank), bf16),
            pltpu.VMEM((pairs, rows, 2 * width), f32),
            pltpu.VMEM((pairs, rows, 2 * width), bf16),
            pltpu.VMEM((pairs, rows, 2 * width), bf16),
            pltpu.VMEM((n, rows, rank), f32),
            pltpu.VMEM((n, rows, rank), bf16),
            pltpu.VMEM((n, rows, rank), f32),
            pltpu.VMEM((n, rows, rank), f32),
            dma((5,)),
            dma((3, 2)), dma((3, 2)),
            dma((2, 2)), dma((2, 2)),
            dma((chunks,)), dma((chunks,)),
            dma((n,)), dma((n,)),
            dma((n,)), dma((n,)),
        ],
        compiler_params=pltpu.CompilerParams(
            collective_id=0, has_side_effects=True, vmem_limit_bytes=56 * 1024 * 1024
        ),
    )(
        vectors, leaf_basis, local_transfer, coupling, near_blocks,
        coupling_source.T, near_source.T, top_target, top_source, top_transfer, top_coupling,
    )


def solution(mesh):
    placed = (
        P("rhs", "leaf"),
        P("leaf", None, None),
        P("leaf", None, None),
        P("leaf", None, None, None),
        P("leaf", None),
        P(),
        P("leaf", None, None),
        P("leaf"),
        P("leaf"),
        P("leaf", "rhs", None, None),
        P("leaf", "rhs"),
    )
    return jax.shard_map(
        shards, mesh=mesh, in_specs=placed, out_specs=P("rhs", "leaf"), check_vma=False
    )
```

```python
import functools

import jax
import jax.numpy as jnp
from jax import lax
from jax.experimental import pallas as pl
from jax.experimental.pallas import tpu as pltpu
from jax.sharding import PartitionSpec as P

MESH = pl.DeviceIdType.MESH
NT = (((1,), (1,)), ((), ()))
NN = (((1,), (0,)), ((), ()))
f32 = jnp.float32
bf16 = jnp.bfloat16


def mm(a, b, dims=NN):
    return lax.dot_general(a, b, dims, preferred_element_type=f32)


def mm_split(a, b, dims):
    high = a.astype(bf16)
    low = (a - high.astype(f32)).astype(bf16)
    return mm(high, b, dims) + mm(low, b, dims)


def level_table(leaf_count):
    layout = []
    first, count, pair = 0, leaf_count, 0
    while count >= 1:
        layout.append((first, count, pair))
        first += count
        pair += max(count // 2, 1)
        count //= 2
    return layout


def loop(count, body, unroll):
    unroll = min(unroll, count)
    while count % unroll:
        unroll -= 1

    def step(i, carry):
        for u in range(unroll):
            body(i * unroll + u)
        return carry

    if count == unroll:
        step(0, 0)
    else:
        lax.fori_loop(0, count // unroll, step, 0)


def kernel(
    roots_n,
    vec, basis_h, trans_h, coup_h, near_h,
    cs, ns, tt, ts, top_t, top_c,
    out,
    vbuf, pts, basis, trans_raw, coup_raw, near, trans_rows, trans, coup,
    cp, halo, cl, field, down, near_own, near_send, near_recv,
    roots, uc, g, top_recv,
    local_sem, vs_sem, vr_sem, hs_sem, hr_sem, ns_sem, nr_sem, rs_sem, rr_sem, ts_sem, tr_sem,
):
    n = roots_n
    leaves = basis.shape[0]
    width = basis.shape[1]
    rows = vec.shape[0]
    layout = level_table(leaves)
    pairs = leaves // 2
    slots = coup_raw.shape[0]
    nodes = trans.shape[0]
    near_slots = near.shape[1]
    top_blocks = top_c.shape[0]
    me = lax.axis_index("leaf")
    mine = lax.axis_index("rhs")
    other = 1 - mine
    has_left, has_right = me > 0, me < n - 1

    def peer_of(i):
        return lax.rem(me + i, n)

    barrier = pltpu.get_barrier_semaphore()

    def greet(i, carry):
        pl.semaphore_signal(barrier, inc=1, device_id=(peer_of(i), mine), device_id_type=MESH)
        return carry

    lax.fori_loop(1, n, greet, 0)
    pl.semaphore_signal(barrier, inc=1, device_id=(me, other), device_id_type=MESH)

    @pl.when(has_left)
    def _():
        pl.semaphore_signal(barrier, inc=1, device_id=(me - 1, other), device_id_type=MESH)

    @pl.when(has_right)
    def _():
        pl.semaphore_signal(barrier, inc=1, device_id=(me + 1, other), device_id_type=MESH)

    local = [
        pltpu.make_async_copy(src, dst, local_sem.at[i])
        for i, (src, dst) in enumerate(
            ((vec, vbuf.at[1, 0]), (basis_h, basis), (trans_h, trans_raw), (near_h, near), (coup_h, coup_raw))
        )
    ]
    for copy in local:
        copy.start()

    pl.semaphore_wait(barrier, n + jnp.where(has_left, 1, 0) + jnp.where(has_right, 1, 0))

    def vec_send(place, half):
        target = (me + (1 - place), mine if half == 0 else other)
        return pltpu.make_async_remote_copy(
            src_ref=vec, dst_ref=vbuf.at[place, half],
            send_sem=vs_sem.at[place, half], recv_sem=vr_sem.at[place, half],
            device_id=target, device_id_type=MESH,
        )

    def halo_send(place, part):
        part_pairs = pl.ds(0, pairs) if part == 0 else pl.ds(pairs, cp.shape[0] - pairs)
        return pltpu.make_async_remote_copy(
            src_ref=cp.at[part_pairs], dst_ref=halo.at[place, part_pairs],
            send_sem=hs_sem.at[place, part], recv_sem=hr_sem.at[place, part],
            device_id=(me + (1 - 2 * place), mine), device_id_type=MESH,
        )

    sends_right, sends_left = has_right, has_left
    vec_send(1, 1).start()

    @pl.when(sends_right)
    def _():
        vec_send(0, 0).start()
        vec_send(0, 1).start()

    @pl.when(sends_left)
    def _():
        vec_send(2, 0).start()
        vec_send(2, 1).start()

    local[0].wait()
    local[1].wait()

    def store_pair(pair_index, node_index, a, b):
        cp[pair_index] = jnp.concatenate([a, b], axis=1)
        cl[node_index] = a
        cl[node_index + 1] = b

    def turned(a, b):
        return jnp.concatenate([a, b], axis=0).astype(f32).T

    def transfer_layout():
        half = width // 2

        def turn(m):
            trans_rows[pl.ds(m, nodes, stride=half), :] = turned(trans_raw[m], trans_raw[m + half])

        def split(t):
            x = trans_rows[pl.ds(pl.multiple_of(t * half, half), half), :].astype(bf16)
            trans[t, :half, :] = x[:, :width]
            trans[t, half:, :] = x[:, width:]

        loop(half, turn, 2)
        lax.fori_loop(0, nodes // 8, lambda i, c: [split(8 * i + u) for u in range(8)] and c, 0)
        for t in range(nodes // 8 * 8, nodes):
            split(t)

    def coupling_layout():
        per = slots // 2
        for k in range(per):
            def turn(m):
                coup[pl.ds(k * width + m, nodes, stride=per * width), :] = turned(coup_raw[k, m], coup_raw[k + per, m])

            loop(width, turn, 2)

    def leaf_up(p):
        x = vbuf[1, 0, :, pl.ds(pl.multiple_of(p * 2 * width, 2 * width), 2 * width)]
        x0, x1 = x[:, :width], x[:, width:]
        c0 = mm(x0, basis[2 * p]).astype(bf16)
        c1 = mm(x1, basis[2 * p + 1]).astype(bf16)
        store_pair(p, leaves + 2 * p, c0, c1)

    loop(pairs, leaf_up, 4)

    @pl.when(sends_right)
    def _():
        halo_send(0, 0).start()

    @pl.when(sends_left)
    def _():
        halo_send(1, 0).start()

    local[2].wait()
    transfer_layout()
    for height in range(1, len(layout)):
        below_first, below_count, below_pair = layout[height - 1]
        first, count, pair = layout[height]

        def lift(q):
            w = trans[pl.ds(below_first + 2 * q, 2)].reshape(2 * width, width)
            return mm(cp[below_pair + q], w).astype(bf16)

        if count > 1:
            def up(p):
                store_pair(pair + p, 3 * first + count + 2 * p, lift(2 * p), lift(2 * p + 1))

            loop(count // 2, up, 4)
        else:
            c = lift(0)
            cp[pair] = jnp.concatenate([c, c], axis=1)
            cl[3 * first + count] = c
    root_row = layout[-1][0]
    root_pair = layout[-1][2]
    root_term = mm(cp[root_pair][:, :width], trans[root_row])
    roots[me] = root_term

    def root_copy(i):
        return pltpu.make_async_remote_copy(
            src_ref=roots.at[me], dst_ref=roots.at[me],
            send_sem=rs_sem.at[i], recv_sem=rr_sem.at[me],
            device_id=(peer_of(i), mine), device_id_type=MESH,
        )

    def root_recv(i):
        source = peer_of(i)
        return pltpu.make_async_remote_copy(
            src_ref=roots.at[source], dst_ref=roots.at[source],
            send_sem=rs_sem.at[i], recv_sem=rr_sem.at[source],
            device_id=(source, mine), device_id_type=MESH,
        )

    def send_roots(i, carry):
        root_copy(i).start()
        return carry

    lax.fori_loop(1, n, send_roots, 0)

    @pl.when(sends_right)
    def _():
        halo_send(0, 1).start()

    @pl.when(sends_left)
    def _():
        halo_send(1, 1).start()

    local[4].wait()
    coupling_layout()

    def unpack_points(place, half):
        def body(p):
            x = vbuf[place, half, :, pl.ds(pl.multiple_of(p * 2 * width, 2 * width), 2 * width)]
            pts[place * leaves + 2 * p, half * rows:(half + 1) * rows, :] = x[:, :width]
            pts[place * leaves + 2 * p + 1, half * rows:(half + 1) * rows, :] = x[:, width:]

        loop(pairs, body, 8)

    unpack_points(1, 0)

    @pl.when(jnp.logical_not(has_left))
    def _():
        vbuf[0] = jnp.zeros(vbuf.shape[1:], bf16)
        halo[0] = jnp.zeros(halo.shape[1:], bf16)

    @pl.when(jnp.logical_not(has_right))
    def _():
        vbuf[2] = jnp.zeros(vbuf.shape[1:], bf16)
        halo[1] = jnp.zeros(halo.shape[1:], bf16)

    vec_send(1, 1).wait_recv()
    unpack_points(1, 1)
    for half in range(2):
        @pl.when(has_left)
        def _():
            vec_send(0, half).wait_recv()

        unpack_points(0, half)

        @pl.when(has_right)
        def _():
            vec_send(2, half).wait_recv()

        unpack_points(2, half)

    local[3].wait()
    leaf_base = (me - 1) * leaves

    def near_leaf(i):
        total = None
        for j in range(near_slots):
            term = mm(pts[jnp.clip(ns[j, i] - leaf_base, 0, 3 * leaves - 1)], near[i, j], NT)
            total = term if total is None else total + term
        return total

    def near_pair(p):
        both = jnp.concatenate([near_leaf(2 * p), near_leaf(2 * p + 1)], axis=1)
        near_own[p] = both[:rows]
        near_send[p] = both[rows:].astype(bf16)

    chunks = near_recv_chunks = ns_sem.shape[0]
    chunk = pairs // chunks

    def near_copy(c):
        part = pl.ds(c * chunk, chunk)
        return pltpu.make_async_remote_copy(
            src_ref=near_send.at[part], dst_ref=near_recv.at[part],
            send_sem=ns_sem.at[c], recv_sem=nr_sem.at[c],
            device_id=(me, other), device_id_type=MESH,
        )

    for c in range(chunks):
        loop(chunk, lambda p: near_pair(c * chunk + p), 2)
        near_copy(c).start()

    def recv_roots(i, carry):
        root_recv(i).wait_recv()
        return carry

    lax.fori_loop(1, n, recv_roots, 0)
    half_n = n // 2
    uc[0] = jnp.zeros(uc.shape[1:], bf16)
    uc[1] = jnp.zeros(uc.shape[1:], bf16)
    loop(half_n, lambda j: uc.__setitem__(half_n + j, (roots[2 * j] + roots[2 * j + 1]).astype(bf16)), 4)
    size = half_n // 2
    while size >= 2:
        def upper_up(j):
            h = size + j
            x = mm(uc[2 * h], top_t[2 * h - 2]) + mm(uc[2 * h + 1], top_t[2 * h - 1])
            uc[h] = x.astype(bf16)

        loop(size, upper_up, 4)
        size //= 2
    terms = [mm(uc[ts[b]], top_c[b]) for b in range(top_blocks)]

    def upper_gather(j):
        h = j + 2
        total = None
        for b in range(top_blocks):
            term = terms[b] * (tt[b] == h).astype(f32)
            total = term if total is None else total + term
        g[h] = total

    loop(n - 2, upper_gather, 2)
    size = 2
    while size < half_n:
        def upper_down(j):
            h = size + j
            w = top_t[pl.ds(2 * h - 2, 2)].reshape(2 * width, width)
            x = mm_split(g[h], w, NT)
            g[2 * h] = g[2 * h] + x[:, :width]
            g[2 * h + 1] = g[2 * h + 1] + x[:, width:]

        loop(size, upper_down, 4)
        size *= 2

    def top_copy(i):
        peer = peer_of(i)
        return pltpu.make_async_remote_copy(
            src_ref=g.at[half_n + peer // 2], dst_ref=top_recv.at[me],
            send_sem=ts_sem.at[i], recv_sem=tr_sem.at[me],
            device_id=(peer, mine), device_id_type=MESH,
        )

    def top_wait(i):
        source = peer_of(i)
        return pltpu.make_async_remote_copy(
            src_ref=g.at[half_n + source // 2], dst_ref=top_recv.at[source],
            send_sem=ts_sem.at[i], recv_sem=tr_sem.at[source],
            device_id=(source, mine), device_id_type=MESH,
        )

    def send_top(i, carry):
        top_copy(i).start()
        return carry

    lax.fori_loop(1, n, send_top, 0)

    for part in range(2):
        @pl.when(has_left)
        def _():
            halo_send(0, part).wait_recv()

        @pl.when(has_right)
        def _():
            halo_send(1, part).wait_recv()

    for first, count, pair in layout:
        for place in range(2):
            base = 3 * first + 2 * place * count
            if count > 1:
                def unpack(p):
                    x = halo[place, pair + p]
                    cl[base + 2 * p] = x[:, :width]
                    cl[base + 2 * p + 1] = x[:, width:]

                loop(count // 2, unpack, 8)
            else:
                cl[base] = halo[place, pair][:, :width]

    depth = slots // 2 * width
    left_half = lax.broadcasted_iota(jnp.int32, (rows, 2 * width), 1) < width
    for first, count, pair in layout:
        base = 3 * first - (me - 1) * count

        def node_terms(t):
            c = [cl[jnp.clip(base + cs[k, first + t], 0, cl.shape[0] - 1)] for k in range(slots)]
            per = slots // 2
            x = jnp.concatenate(
                [jnp.concatenate(c[:per], axis=1), jnp.concatenate(c[per:], axis=1)], axis=0
            )
            w = coup[pl.ds(pl.multiple_of((first + t) * depth, depth), depth), :].astype(bf16)
            r = mm(x, w)
            return r[:rows], r[rows:]

        if count > 1:
            def pair_field(p):
                a0, b0 = node_terms(2 * p)
                a1, b1 = node_terms(2 * p + 1)
                even = a0 + pltpu.roll(b0, width, 1)
                odd = pltpu.roll(a1, width, 1) + b1
                field[pair + p] = jnp.where(left_half, even, odd)

            loop(count // 2, pair_field, 4)
        else:
            a0, b0 = node_terms(0)
            root_field = (a0 + pltpu.roll(b0, width, 1))[:, :width]

    def recv_top(i, total):
        top_wait(i).wait_recv()
        return total + top_recv[peer_of(i)]

    parent = lax.fori_loop(1, n, recv_top, g[half_n + me // 2])
    root_down = (root_field + mm_split(parent, trans[root_row], NT)).astype(bf16)

    def step_down(height, q, x):
        first, count, pair = layout[height]
        w = trans[pl.ds(first + 2 * q, 2)].reshape(2 * width, width)
        return (field[pair + q] + mm(x, w, NT)).astype(bf16)

    top_height = len(layout) - 2
    down[layout[top_height][2]] = step_down(top_height, 0, root_down)
    for height in range(top_height - 1, 0, -1):
        pair = layout[height][2]
        above = layout[height + 1][2]

        def descend(p):
            x = down[above + p]
            down[pair + 2 * p] = step_down(height, 2 * p, x[:, :width])
            down[pair + 2 * p + 1] = step_down(height, 2 * p + 1, x[:, width:])

        loop(layout[height][1] // 4, descend, 4)

    for c in range(chunks):
        near_copy(c).wait_recv()
    above = layout[1][2]

    def leaf_pair(p, x):
        y = step_down(0, p, x)
        far = jnp.concatenate(
            [mm(y[:, :width], basis[2 * p], NT), mm(y[:, width:], basis[2 * p + 1], NT)], axis=1
        )
        total = far + (near_own[p] + near_recv[p].astype(f32))
        out[:, pl.ds(pl.multiple_of(p * 2 * width, 2 * width), 2 * width)] = total.astype(bf16)

    def leaf_down(p):
        x = down[above + p]
        leaf_pair(2 * p, x[:, :width])
        leaf_pair(2 * p + 1, x[:, width:])

    loop(pairs // 2, leaf_down, 2)

    vec_send(1, 1).wait_send()

    @pl.when(sends_right)
    def _():
        for part in range(2):
            vec_send(0, part).wait_send()
            halo_send(0, part).wait_send()

    @pl.when(sends_left)
    def _():
        for part in range(2):
            vec_send(2, part).wait_send()
            halo_send(1, part).wait_send()

    for c in range(chunks):
        near_copy(c).wait_send()

    def end_sends(i, carry):
        root_copy(i).wait_send()
        top_copy(i).wait_send()
        return carry

    lax.fori_loop(1, n, end_sends, 0)


def shards(
    vectors, leaf_basis, local_transfer, coupling, coupling_source,
    top_transfer, top_coupling, top_target, top_source, near_blocks, near_source,
):
    n = lax.axis_size("leaf")
    rows = vectors.shape[0]
    leaves, width, rank = leaf_basis.shape
    nodes = local_transfer.shape[0]
    slots = coupling.shape[1]
    pairs = leaves // 2
    pair_total = leaves
    chunks = 4
    any_spec = pl.BlockSpec(memory_space=pl.ANY)
    smem = pl.BlockSpec(memory_space=pltpu.SMEM)
    vmem = pl.BlockSpec(memory_space=pltpu.VMEM)
    dma = pltpu.SemaphoreType.DMA
    return pl.pallas_call(
        functools.partial(kernel, n),
        out_shape=jax.ShapeDtypeStruct(vectors.shape, bf16),
        in_specs=[any_spec] * 5 + [smem] * 4 + [vmem] * 2,
        out_specs=vmem,
        scratch_shapes=[
            pltpu.VMEM((3, 2) + vectors.shape, bf16),
            pltpu.VMEM((3 * leaves, 2 * rows, width), bf16),
            pltpu.VMEM(leaf_basis.shape, bf16),
            pltpu.VMEM((width, rank, nodes), bf16),
            pltpu.VMEM((slots, rank, rank, nodes), bf16),
            pltpu.VMEM(near_blocks.shape, bf16),
            pltpu.VMEM((nodes * rank // 2, 2 * rank), f32),
            pltpu.VMEM(local_transfer.shape, bf16),
            pltpu.VMEM((nodes * slots // 2 * rank, 2 * rank), f32),
            pltpu.VMEM((pair_total, rows, 2 * rank), bf16),
            pltpu.VMEM((2, pair_total, rows, 2 * rank), bf16),
            pltpu.VMEM((3 * nodes, rows, rank), bf16),
            pltpu.VMEM((pair_total, rows, 2 * rank), f32),
            pltpu.VMEM((pair_total, rows, 2 * rank), bf16),
            pltpu.VMEM((pairs, rows, 2 * width), f32),
            pltpu.VMEM((pairs, rows, 2 * width), bf16),
            pltpu.VMEM((pairs, rows, 2 * width), bf16),
            pltpu.VMEM((n, rows, rank), f32),
            pltpu.VMEM((n, rows, rank), bf16),
            pltpu.VMEM((n, rows, rank), f32),
            pltpu.VMEM((n, rows, rank), f32),
            dma((5,)),
            dma((3, 2)), dma((3, 2)),
            dma((2, 2)), dma((2, 2)),
            dma((chunks,)), dma((chunks,)),
            dma((n,)), dma((n,)),
            dma((n,)), dma((n,)),
        ],
        compiler_params=pltpu.CompilerParams(
            collective_id=0, has_side_effects=True, vmem_limit_bytes=56 * 1024 * 1024
        ),
    )(
        vectors, leaf_basis, local_transfer.transpose(1, 2, 0), coupling.transpose(1, 2, 3, 0), near_blocks,
        coupling_source.T, near_source.T, top_target, top_source, top_transfer, top_coupling,
    )


def solution(mesh):
    placed = (
        P("rhs", "leaf"),
        P("leaf", None, None),
        P("leaf", None, None),
        P("leaf", None, None, None),
        P("leaf", None),
        P(),
        P("leaf", None, None),
        P("leaf"),
        P("leaf"),
        P("leaf", "rhs", None, None),
        P("leaf", "rhs"),
    )
    return jax.shard_map(
        shards, mesh=mesh, in_specs=placed, out_specs=P("rhs", "leaf"), check_vma=False
    )
```

```python
import functools

import jax
import jax.numpy as jnp
from jax import lax
from jax.experimental import pallas as pl
from jax.experimental.pallas import tpu as pltpu
from jax.sharding import PartitionSpec as P

MESH = pl.DeviceIdType.MESH
NT = (((1,), (1,)), ((), ()))
NN = (((1,), (0,)), ((), ()))
f32 = jnp.float32
bf16 = jnp.bfloat16


def mm(a, b, dims=NN):
    return lax.dot_general(a, b, dims, preferred_element_type=f32)


def mm_split(a, b, dims):
    high = a.astype(bf16)
    low = (a - high.astype(f32)).astype(bf16)
    return mm(high, b, dims) + mm(low, b, dims)


def level_table(leaf_count):
    layout = []
    first, count, pair = 0, leaf_count, 0
    while count >= 1:
        layout.append((first, count, pair))
        first += count
        pair += max(count // 2, 1)
        count //= 2
    return layout


def loop(count, body, unroll):
    unroll = min(unroll, count)
    while count % unroll:
        unroll -= 1

    def step(i, carry):
        for u in range(unroll):
            body(i * unroll + u)
        return carry

    if count == unroll:
        step(0, 0)
    else:
        lax.fori_loop(0, count // unroll, step, 0)


def kernel(
    roots_n,
    vec, basis_h, trans_h, coup_h, near_h,
    cs, ns, tt, ts, top_t, top_c,
    out,
    vbuf, pts, basis, trans_raw, coup_raw, near, trans_rows, trans, coup,
    cp, halo, cl, field, down, near_own, near_send, near_recv,
    roots, uc, g, top_recv,
    local_sem, vs_sem, vr_sem, hs_sem, hr_sem, ns_sem, nr_sem, rs_sem, rr_sem, ts_sem, tr_sem,
):
    n = roots_n
    leaves = basis.shape[0]
    width = basis.shape[1]
    rows = vec.shape[0]
    layout = level_table(leaves)
    pairs = leaves // 2
    slots = coup_raw.shape[0]
    nodes = trans.shape[0]
    near_slots = near.shape[1]
    top_blocks = top_c.shape[0]
    me = lax.axis_index("leaf")
    mine = lax.axis_index("rhs")
    other = 1 - mine
    has_left, has_right = me > 0, me < n - 1
    odd = lax.rem(me, 2)
    buddy = me + 1 - 2 * odd
    far = me - 1 + 2 * odd
    has_far = jnp.logical_and(far >= 0, far < n)

    def peer_of(i):
        return lax.rem(me + i, n)

    barrier = pltpu.get_barrier_semaphore()

    def greet(i, carry):
        pl.semaphore_signal(barrier, inc=1, device_id=(peer_of(i), mine), device_id_type=MESH)
        return carry

    lax.fori_loop(1, n, greet, 0)
    pl.semaphore_signal(barrier, inc=1, device_id=(me, other), device_id_type=MESH)

    local = [
        pltpu.make_async_copy(src, dst, local_sem.at[i])
        for i, (src, dst) in enumerate(
            ((vec, vbuf.at[0, 0]), (basis_h, basis), (trans_h, trans_raw), (near_h, near), (coup_h, coup_raw))
        )
    ]
    for copy in local:
        copy.start()

    pl.semaphore_wait(barrier, n)

    def vec_send(kind, half):
        source = vec
        if half == 1 and kind > 0:
            source = vbuf.at[0, 1] if kind == 1 else vbuf.at[2, 0]
        if kind == 1:
            target = (buddy, mine)
        elif kind == 2 and half == 0:
            target = (far, mine)
        else:
            target = (me, other)
        return pltpu.make_async_remote_copy(
            src_ref=source, dst_ref=vbuf.at[kind, half],
            send_sem=vs_sem.at[kind, half], recv_sem=vr_sem.at[kind, half],
            device_id=target, device_id_type=MESH,
        )

    def halo_send(place, part):
        part_pairs = pl.ds(0, pairs) if part == 0 else pl.ds(pairs, cp.shape[0] - pairs)
        return pltpu.make_async_remote_copy(
            src_ref=cp.at[part_pairs], dst_ref=halo.at[place, part_pairs],
            send_sem=hs_sem.at[place, part], recv_sem=hr_sem.at[place, part],
            device_id=(me + (1 - 2 * place), mine), device_id_type=MESH,
        )

    sends_right, sends_left = has_right, has_left
    vec_send(0, 1).start()
    vec_send(1, 0).start()

    @pl.when(has_far)
    def _():
        vec_send(2, 0).start()

    local[0].wait()
    local[1].wait()

    def store_pair(pair_index, node_index, a, b):
        cp[pair_index] = jnp.concatenate([a, b], axis=1)
        cl[node_index] = a
        cl[node_index + 1] = b

    def turned(a, b):
        return jnp.concatenate([a, b], axis=0).astype(f32).T

    def transfer_layout():
        half = width // 2

        def turn(m):
            trans_rows[pl.ds(m, nodes, stride=half), :] = turned(trans_raw[m], trans_raw[m + half])

        def split(t):
            x = trans_rows[pl.ds(pl.multiple_of(t * half, half), half), :].astype(bf16)
            trans[t, :half, :] = x[:, :width]
            trans[t, half:, :] = x[:, width:]

        loop(half, turn, 2)
        lax.fori_loop(0, nodes // 8, lambda i, c: [split(8 * i + u) for u in range(8)] and c, 0)
        for t in range(nodes // 8 * 8, nodes):
            split(t)

    def coupling_layout():
        per = slots // 2
        for k in range(per):
            def turn(m):
                coup[pl.ds(k * width + m, nodes, stride=per * width), :] = turned(coup_raw[k, m], coup_raw[k + per, m])

            loop(width, turn, 2)

    def leaf_up(p):
        x = vbuf[0, 0, :, pl.ds(pl.multiple_of(p * 2 * width, 2 * width), 2 * width)]
        x0, x1 = x[:, :width], x[:, width:]
        c0 = mm(x0, basis[2 * p]).astype(bf16)
        c1 = mm(x1, basis[2 * p + 1]).astype(bf16)
        store_pair(p, leaves + 2 * p, c0, c1)

    loop(pairs, leaf_up, 4)

    @pl.when(sends_right)
    def _():
        halo_send(0, 0).start()

    @pl.when(sends_left)
    def _():
        halo_send(1, 0).start()

    local[2].wait()
    transfer_layout()
    for height in range(1, len(layout)):
        below_first, below_count, below_pair = layout[height - 1]
        first, count, pair = layout[height]

        def lift(q):
            w = trans[pl.ds(below_first + 2 * q, 2)].reshape(2 * width, width)
            return mm(cp[below_pair + q], w).astype(bf16)

        if count > 1:
            def up(p):
                store_pair(pair + p, 3 * first + count + 2 * p, lift(2 * p), lift(2 * p + 1))

            loop(count // 2, up, 4)
        else:
            c = lift(0)
            cp[pair] = jnp.concatenate([c, c], axis=1)
            cl[3 * first + count] = c
    root_row = layout[-1][0]
    root_pair = layout[-1][2]
    root_term = mm(cp[root_pair][:, :width], trans[root_row])
    roots[me] = root_term

    def root_copy(i):
        return pltpu.make_async_remote_copy(
            src_ref=roots.at[me], dst_ref=roots.at[me],
            send_sem=rs_sem.at[i], recv_sem=rr_sem.at[me],
            device_id=(peer_of(i), mine), device_id_type=MESH,
        )

    def root_recv(i):
        source = peer_of(i)
        return pltpu.make_async_remote_copy(
            src_ref=roots.at[source], dst_ref=roots.at[source],
            send_sem=rs_sem.at[i], recv_sem=rr_sem.at[source],
            device_id=(source, mine), device_id_type=MESH,
        )

    def send_roots(i, carry):
        root_copy(i).start()
        return carry

    lax.fori_loop(1, n, send_roots, 0)

    @pl.when(sends_right)
    def _():
        halo_send(0, 1).start()

    @pl.when(sends_left)
    def _():
        halo_send(1, 1).start()

    vec_send(0, 1).wait_recv()
    vec_send(1, 1).start()

    @pl.when(has_far)
    def _():
        vec_send(2, 0).wait_recv()
        vec_send(2, 1).start()

    local[4].wait()
    coupling_layout()

    def unpack_points(kind, half):
        place = (1, 2 - 2 * odd, 2 * odd)[kind]

        def body(p):
            x = vbuf[kind, half, :, pl.ds(pl.multiple_of(p * 2 * width, 2 * width), 2 * width)]
            pts[place * leaves + 2 * p, half * rows:(half + 1) * rows, :] = x[:, :width]
            pts[place * leaves + 2 * p + 1, half * rows:(half + 1) * rows, :] = x[:, width:]

        loop(pairs, body, 8)

    @pl.when(jnp.logical_not(has_far))
    def _():
        vbuf[2] = jnp.zeros(vbuf.shape[1:], bf16)

    @pl.when(jnp.logical_not(has_left))
    def _():
        halo[0] = jnp.zeros(halo.shape[1:], bf16)

    @pl.when(jnp.logical_not(has_right))
    def _():
        halo[1] = jnp.zeros(halo.shape[1:], bf16)

    unpack_points(0, 0)
    unpack_points(0, 1)
    vec_send(1, 0).wait_recv()
    unpack_points(1, 0)
    unpack_points(2, 0)
    vec_send(1, 1).wait_recv()
    unpack_points(1, 1)

    @pl.when(has_far)
    def _():
        vec_send(2, 1).wait_recv()

    unpack_points(2, 1)
    local[3].wait()
    leaf_base = (me - 1) * leaves

    def near_leaf(i):
        total = None
        for j in range(near_slots):
            term = mm(pts[jnp.clip(ns[j, i] - leaf_base, 0, 3 * leaves - 1)], near[i, j], NT)
            total = term if total is None else total + term
        return total

    def near_pair(p):
        both = jnp.concatenate([near_leaf(2 * p), near_leaf(2 * p + 1)], axis=1)
        near_own[p] = both[:rows]
        near_send[p] = both[rows:].astype(bf16)

    chunks = near_recv_chunks = ns_sem.shape[0]
    chunk = pairs // chunks

    def near_copy(c):
        part = pl.ds(c * chunk, chunk)
        return pltpu.make_async_remote_copy(
            src_ref=near_send.at[part], dst_ref=near_recv.at[part],
            send_sem=ns_sem.at[c], recv_sem=nr_sem.at[c],
            device_id=(me, other), device_id_type=MESH,
        )

    for c in range(chunks):
        loop(chunk, lambda p: near_pair(c * chunk + p), 2)
        near_copy(c).start()

    def recv_roots(i, carry):
        root_recv(i).wait_recv()
        return carry

    lax.fori_loop(1, n, recv_roots, 0)
    half_n = n // 2
    uc[0] = jnp.zeros(uc.shape[1:], bf16)
    uc[1] = jnp.zeros(uc.shape[1:], bf16)
    loop(half_n, lambda j: uc.__setitem__(half_n + j, (roots[2 * j] + roots[2 * j + 1]).astype(bf16)), 4)
    size = half_n // 2
    while size >= 2:
        def upper_up(j):
            h = size + j
            x = mm(uc[2 * h], top_t[2 * h - 2]) + mm(uc[2 * h + 1], top_t[2 * h - 1])
            uc[h] = x.astype(bf16)

        loop(size, upper_up, 4)
        size //= 2
    terms = [mm(uc[ts[b]], top_c[b]) for b in range(top_blocks)]

    def upper_gather(j):
        h = j + 2
        total = None
        for b in range(top_blocks):
            term = terms[b] * (tt[b] == h).astype(f32)
            total = term if total is None else total + term
        g[h] = total

    loop(n - 2, upper_gather, 2)
    size = 2
    while size < half_n:
        def upper_down(j):
            h = size + j
            w = top_t[pl.ds(2 * h - 2, 2)].reshape(2 * width, width)
            x = mm_split(g[h], w, NT)
            g[2 * h] = g[2 * h] + x[:, :width]
            g[2 * h + 1] = g[2 * h + 1] + x[:, width:]

        loop(size, upper_down, 4)
        size *= 2

    def top_copy(i):
        peer = peer_of(i)
        return pltpu.make_async_remote_copy(
            src_ref=g.at[half_n + peer // 2], dst_ref=top_recv.at[me],
            send_sem=ts_sem.at[i], recv_sem=tr_sem.at[me],
            device_id=(peer, mine), device_id_type=MESH,
        )

    def top_wait(i):
        source = peer_of(i)
        return pltpu.make_async_remote_copy(
            src_ref=g.at[half_n + source // 2], dst_ref=top_recv.at[source],
            send_sem=ts_sem.at[i], recv_sem=tr_sem.at[source],
            device_id=(source, mine), device_id_type=MESH,
        )

    def send_top(i, carry):
        top_copy(i).start()
        return carry

    lax.fori_loop(1, n, send_top, 0)

    for part in range(2):
        @pl.when(has_left)
        def _():
            halo_send(0, part).wait_recv()

        @pl.when(has_right)
        def _():
            halo_send(1, part).wait_recv()

    for first, count, pair in layout:
        for place in range(2):
            base = 3 * first + 2 * place * count
            if count > 1:
                def unpack(p):
                    x = halo[place, pair + p]
                    cl[base + 2 * p] = x[:, :width]
                    cl[base + 2 * p + 1] = x[:, width:]

                loop(count // 2, unpack, 8)
            else:
                cl[base] = halo[place, pair][:, :width]

    depth = slots // 2 * width
    left_half = lax.broadcasted_iota(jnp.int32, (rows, 2 * width), 1) < width
    for first, count, pair in layout:
        base = 3 * first - (me - 1) * count

        def node_terms(t):
            c = [cl[jnp.clip(base + cs[k, first + t], 0, cl.shape[0] - 1)] for k in range(slots)]
            per = slots // 2
            x = jnp.concatenate(
                [jnp.concatenate(c[:per], axis=1), jnp.concatenate(c[per:], axis=1)], axis=0
            )
            w = coup[pl.ds(pl.multiple_of((first + t) * depth, depth), depth), :].astype(bf16)
            r = mm(x, w)
            return r[:rows], r[rows:]

        if count > 1:
            def pair_field(p):
                a0, b0 = node_terms(2 * p)
                a1, b1 = node_terms(2 * p + 1)
                even = a0 + pltpu.roll(b0, width, 1)
                uneven = pltpu.roll(a1, width, 1) + b1
                field[pair + p] = jnp.where(left_half, even, uneven)

            loop(count // 2, pair_field, 4)
        else:
            a0, b0 = node_terms(0)
            root_field = (a0 + pltpu.roll(b0, width, 1))[:, :width]

    def recv_top(i, total):
        top_wait(i).wait_recv()
        return total + top_recv[peer_of(i)]

    parent = lax.fori_loop(1, n, recv_top, g[half_n + me // 2])
    root_down = (root_field + mm_split(parent, trans[root_row], NT)).astype(bf16)

    def step_down(height, q, x):
        first, count, pair = layout[height]
        w = trans[pl.ds(first + 2 * q, 2)].reshape(2 * width, width)
        return (field[pair + q] + mm(x, w, NT)).astype(bf16)

    top_height = len(layout) - 2
    down[layout[top_height][2]] = step_down(top_height, 0, root_down)
    for height in range(top_height - 1, 0, -1):
        pair = layout[height][2]
        above = layout[height + 1][2]

        def descend(p):
            x = down[above + p]
            down[pair + 2 * p] = step_down(height, 2 * p, x[:, :width])
            down[pair + 2 * p + 1] = step_down(height, 2 * p + 1, x[:, width:])

        loop(layout[height][1] // 4, descend, 4)

    for c in range(chunks):
        near_copy(c).wait_recv()
    above = layout[1][2]

    def leaf_pair(p, x):
        y = step_down(0, p, x)
        far = jnp.concatenate(
            [mm(y[:, :width], basis[2 * p], NT), mm(y[:, width:], basis[2 * p + 1], NT)], axis=1
        )
        total = far + (near_own[p] + near_recv[p].astype(f32))
        out[:, pl.ds(pl.multiple_of(p * 2 * width, 2 * width), 2 * width)] = total.astype(bf16)

    def leaf_down(p):
        x = down[above + p]
        leaf_pair(2 * p, x[:, :width])
        leaf_pair(2 * p + 1, x[:, width:])

    loop(pairs // 2, leaf_down, 2)

    vec_send(0, 1).wait_send()
    vec_send(1, 0).wait_send()
    vec_send(1, 1).wait_send()

    @pl.when(has_far)
    def _():
        vec_send(2, 0).wait_send()
        vec_send(2, 1).wait_send()

    @pl.when(sends_right)
    def _():
        halo_send(0, 0).wait_send()
        halo_send(0, 1).wait_send()

    @pl.when(sends_left)
    def _():
        halo_send(1, 0).wait_send()
        halo_send(1, 1).wait_send()

    for c in range(chunks):
        near_copy(c).wait_send()

    def end_sends(i, carry):
        root_copy(i).wait_send()
        top_copy(i).wait_send()
        return carry

    lax.fori_loop(1, n, end_sends, 0)


def shards(
    vectors, leaf_basis, local_transfer, coupling, coupling_source,
    top_transfer, top_coupling, top_target, top_source, near_blocks, near_source,
):
    n = lax.axis_size("leaf")
    rows = vectors.shape[0]
    leaves, width, rank = leaf_basis.shape
    nodes = local_transfer.shape[0]
    slots = coupling.shape[1]
    pairs = leaves // 2
    pair_total = leaves
    chunks = 4
    any_spec = pl.BlockSpec(memory_space=pl.ANY)
    smem = pl.BlockSpec(memory_space=pltpu.SMEM)
    vmem = pl.BlockSpec(memory_space=pltpu.VMEM)
    dma = pltpu.SemaphoreType.DMA
    return pl.pallas_call(
        functools.partial(kernel, n),
        out_shape=jax.ShapeDtypeStruct(vectors.shape, bf16),
        in_specs=[any_spec] * 5 + [smem] * 4 + [vmem] * 2,
        out_specs=vmem,
        scratch_shapes=[
            pltpu.VMEM((3, 2) + vectors.shape, bf16),
            pltpu.VMEM((3 * leaves, 2 * rows, width), bf16),
            pltpu.VMEM(leaf_basis.shape, bf16),
            pltpu.VMEM((width, rank, nodes), bf16),
            pltpu.VMEM((slots, rank, rank, nodes), bf16),
            pltpu.VMEM(near_blocks.shape, bf16),
            pltpu.VMEM((nodes * rank // 2, 2 * rank), f32),
            pltpu.VMEM(local_transfer.shape, bf16),
            pltpu.VMEM((nodes * slots // 2 * rank, 2 * rank), f32),
            pltpu.VMEM((pair_total, rows, 2 * rank), bf16),
            pltpu.VMEM((2, pair_total, rows, 2 * rank), bf16),
            pltpu.VMEM((3 * nodes, rows, rank), bf16),
            pltpu.VMEM((pair_total, rows, 2 * rank), f32),
            pltpu.VMEM((pair_total, rows, 2 * rank), bf16),
            pltpu.VMEM((pairs, rows, 2 * width), f32),
            pltpu.VMEM((pairs, rows, 2 * width), bf16),
            pltpu.VMEM((pairs, rows, 2 * width), bf16),
            pltpu.VMEM((n, rows, rank), f32),
            pltpu.VMEM((n, rows, rank), bf16),
            pltpu.VMEM((n, rows, rank), f32),
            pltpu.VMEM((n, rows, rank), f32),
            dma((5,)),
            dma((3, 2)), dma((3, 2)),
            dma((2, 2)), dma((2, 2)),
            dma((chunks,)), dma((chunks,)),
            dma((n,)), dma((n,)),
            dma((n,)), dma((n,)),
        ],
        compiler_params=pltpu.CompilerParams(
            collective_id=0, has_side_effects=True, vmem_limit_bytes=56 * 1024 * 1024
        ),
    )(
        vectors, leaf_basis, local_transfer.transpose(1, 2, 0), coupling.transpose(1, 2, 3, 0), near_blocks,
        coupling_source.T, near_source.T, top_target, top_source, top_transfer, top_coupling,
    )


def solution(mesh):
    placed = (
        P("rhs", "leaf"),
        P("leaf", None, None),
        P("leaf", None, None),
        P("leaf", None, None, None),
        P("leaf", None),
        P(),
        P("leaf", None, None),
        P("leaf"),
        P("leaf"),
        P("leaf", "rhs", None, None),
        P("leaf", "rhs"),
    )
    return jax.shard_map(
        shards, mesh=mesh, in_specs=placed, out_specs=P("rhs", "leaf"), check_vma=False
    )
```

```python
import functools

import jax
import jax.numpy as jnp
from jax import lax
from jax.experimental import pallas as pl
from jax.experimental.pallas import tpu as pltpu
from jax.sharding import PartitionSpec as P

MESH = pl.DeviceIdType.MESH
NT = (((1,), (1,)), ((), ()))
NN = (((1,), (0,)), ((), ()))
f32 = jnp.float32
bf16 = jnp.bfloat16


def mm(a, b, dims=NN):
    return lax.dot_general(a, b, dims, preferred_element_type=f32)


def mm_split(a, b, dims):
    high = a.astype(bf16)
    low = (a - high.astype(f32)).astype(bf16)
    return mm(high, b, dims) + mm(low, b, dims)


def level_table(leaf_count):
    layout = []
    first, count, pair = 0, leaf_count, 0
    while count >= 1:
        layout.append((first, count, pair))
        first += count
        pair += max(count // 2, 1)
        count //= 2
    return layout


def loop(count, body, unroll):
    unroll = min(unroll, count)
    while count % unroll:
        unroll -= 1

    def step(i, carry):
        parts = [body(i * unroll + u) for u in range(unroll)]
        if hasattr(parts[0], "__next__"):
            for part in parts:
                next(part)
            for part in parts:
                next(part, None)
        return carry

    if count == unroll:
        step(0, 0)
    else:
        lax.fori_loop(0, count // unroll, step, 0)


def kernel(
    roots_n,
    vec, basis_h, trans_h, coup_h, near_h,
    cs, ns, tt, ts, top_t, top_c,
    out,
    vbuf, pts, basis, trans_raw, coup_raw, near, trans_rows, trans, coup,
    cp, halo, cl, field, down, near_own, near_send, near_recv,
    roots, uc, g, top_recv,
    local_sem, vs_sem, vr_sem, hs_sem, hr_sem, ns_sem, nr_sem, rs_sem, rr_sem, ts_sem, tr_sem,
):
    n = roots_n
    leaves = basis.shape[0]
    width = basis.shape[1]
    rows = vec.shape[0]
    layout = level_table(leaves)
    pairs = leaves // 2
    slots = coup_raw.shape[0]
    nodes = trans.shape[0]
    near_slots = near.shape[1]
    top_blocks = top_c.shape[0]
    me = lax.axis_index("leaf")
    mine = lax.axis_index("rhs")
    other = 1 - mine
    has_left, has_right = me > 0, me < n - 1
    odd = lax.rem(me, 2)
    buddy = me + 1 - 2 * odd
    far = me - 1 + 2 * odd
    has_far = jnp.logical_and(far >= 0, far < n)

    def peer_of(i):
        return lax.rem(me + i, n)

    barrier = pltpu.get_barrier_semaphore()

    def greet(i, carry):
        pl.semaphore_signal(barrier, inc=1, device_id=(peer_of(i), mine), device_id_type=MESH)
        return carry

    lax.fori_loop(1, n, greet, 0)
    pl.semaphore_signal(barrier, inc=1, device_id=(me, other), device_id_type=MESH)

    local = [
        pltpu.make_async_copy(src, dst, local_sem.at[i])
        for i, (src, dst) in enumerate(
            ((vec, vbuf.at[0, 0]), (basis_h, basis), (trans_h, trans_raw), (near_h, near), (coup_h, coup_raw))
        )
    ]
    for copy in local:
        copy.start()

    pl.semaphore_wait(barrier, n)

    def vec_send(kind, half):
        source = vec
        if half == 1 and kind > 0:
            source = vbuf.at[0, 1] if kind == 1 else vbuf.at[2, 0]
        if kind == 1:
            target = (buddy, mine)
        elif kind == 2 and half == 0:
            target = (far, mine)
        else:
            target = (me, other)
        return pltpu.make_async_remote_copy(
            src_ref=source, dst_ref=vbuf.at[kind, half],
            send_sem=vs_sem.at[kind, half], recv_sem=vr_sem.at[kind, half],
            device_id=target, device_id_type=MESH,
        )

    def halo_send(place, part):
        part_pairs = pl.ds(0, pairs) if part == 0 else pl.ds(pairs, cp.shape[0] - pairs)
        return pltpu.make_async_remote_copy(
            src_ref=cp.at[part_pairs], dst_ref=halo.at[place, part_pairs],
            send_sem=hs_sem.at[place, part], recv_sem=hr_sem.at[place, part],
            device_id=(me + (1 - 2 * place), mine), device_id_type=MESH,
        )

    sends_right, sends_left = has_right, has_left
    vec_send(0, 1).start()
    vec_send(1, 0).start()

    @pl.when(has_far)
    def _():
        vec_send(2, 0).start()

    local[0].wait()
    local[1].wait()

    def store_pair(pair_index, node_index, a, b):
        cp[pair_index] = jnp.concatenate([a, b], axis=1)
        cl[node_index] = a
        cl[node_index + 1] = b

    def turned(a, b):
        return jnp.concatenate([a, b], axis=0).astype(f32).T

    def transfer_layout():
        half = width // 2

        def turn(m):
            trans_rows[pl.ds(m, nodes, stride=half), :] = turned(trans_raw[m], trans_raw[m + half])

        def split(t):
            x = trans_rows[pl.ds(pl.multiple_of(t * half, half), half), :].astype(bf16)
            trans[t, :half, :] = x[:, :width]
            trans[t, half:, :] = x[:, width:]

        loop(half, turn, 8)
        whole = nodes // 16 * 16
        loop(whole, split, 16)
        for t in range(whole, nodes):
            split(t)

    def coupling_layout():
        per = slots // 2
        for k in range(per):
            def turn(m):
                coup[pl.ds(k * width + m, nodes, stride=per * width), :] = turned(coup_raw[k, m], coup_raw[k + per, m])

            loop(width, turn, 8)

    def leaf_up(p):
        x = vbuf[0, 0, :, pl.ds(pl.multiple_of(p * 2 * width, 2 * width), 2 * width)]
        x0, x1 = x[:, :width], x[:, width:]
        c0 = mm(x0, basis[2 * p]).astype(bf16)
        c1 = mm(x1, basis[2 * p + 1]).astype(bf16)
        store_pair(p, leaves + 2 * p, c0, c1)

    loop(pairs, leaf_up, 16)

    @pl.when(sends_right)
    def _():
        halo_send(0, 0).start()

    @pl.when(sends_left)
    def _():
        halo_send(1, 0).start()

    local[2].wait()
    transfer_layout()
    for height in range(1, len(layout)):
        below_first, below_count, below_pair = layout[height - 1]
        first, count, pair = layout[height]

        def lift(q):
            w = trans[pl.ds(below_first + 2 * q, 2)].reshape(2 * width, width)
            return mm(cp[below_pair + q], w).astype(bf16)

        if count > 1:
            def up(p):
                a, b = lift(2 * p), lift(2 * p + 1)
                yield
                store_pair(pair + p, 3 * first + count + 2 * p, a, b)

            loop(count // 2, up, 16)
        else:
            c = lift(0)
            cp[pair] = jnp.concatenate([c, c], axis=1)
            cl[3 * first + count] = c
    root_row = layout[-1][0]
    root_pair = layout[-1][2]
    root_term = mm(cp[root_pair][:, :width], trans[root_row])
    roots[me] = root_term

    def root_copy(i):
        return pltpu.make_async_remote_copy(
            src_ref=roots.at[me], dst_ref=roots.at[me],
            send_sem=rs_sem.at[i], recv_sem=rr_sem.at[me],
            device_id=(peer_of(i), mine), device_id_type=MESH,
        )

    def root_recv(i):
        source = peer_of(i)
        return pltpu.make_async_remote_copy(
            src_ref=roots.at[source], dst_ref=roots.at[source],
            send_sem=rs_sem.at[i], recv_sem=rr_sem.at[source],
            device_id=(source, mine), device_id_type=MESH,
        )

    def send_roots(i, carry):
        root_copy(i).start()
        return carry

    lax.fori_loop(1, n, send_roots, 0)

    @pl.when(sends_right)
    def _():
        halo_send(0, 1).start()

    @pl.when(sends_left)
    def _():
        halo_send(1, 1).start()

    vec_send(0, 1).wait_recv()
    vec_send(1, 1).start()

    @pl.when(has_far)
    def _():
        vec_send(2, 0).wait_recv()
        vec_send(2, 1).start()

    local[4].wait()
    coupling_layout()

    def unpack_points(kind, half):
        place = (1, 2 - 2 * odd, 2 * odd)[kind]

        def body(p):
            x = vbuf[kind, half, :, pl.ds(pl.multiple_of(p * 2 * width, 2 * width), 2 * width)]
            pts[place * leaves + 2 * p, half * rows:(half + 1) * rows, :] = x[:, :width]
            pts[place * leaves + 2 * p + 1, half * rows:(half + 1) * rows, :] = x[:, width:]

        loop(pairs, body, 16)

    @pl.when(jnp.logical_not(has_far))
    def _():
        vbuf[2] = jnp.zeros(vbuf.shape[1:], bf16)

    @pl.when(jnp.logical_not(has_left))
    def _():
        halo[0] = jnp.zeros(halo.shape[1:], bf16)

    @pl.when(jnp.logical_not(has_right))
    def _():
        halo[1] = jnp.zeros(halo.shape[1:], bf16)

    unpack_points(0, 0)
    unpack_points(0, 1)
    vec_send(1, 0).wait_recv()
    unpack_points(1, 0)
    unpack_points(2, 0)
    vec_send(1, 1).wait_recv()
    unpack_points(1, 1)

    @pl.when(has_far)
    def _():
        vec_send(2, 1).wait_recv()

    unpack_points(2, 1)
    local[3].wait()
    leaf_base = (me - 1) * leaves

    def near_leaf(i):
        total = None
        for j in range(near_slots):
            term = mm(pts[jnp.clip(ns[j, i] - leaf_base, 0, 3 * leaves - 1)], near[i, j], NT)
            total = term if total is None else total + term
        return total

    def near_pair(p):
        both = jnp.concatenate([near_leaf(2 * p), near_leaf(2 * p + 1)], axis=1)
        near_own[p] = both[:rows]
        near_send[p] = both[rows:].astype(bf16)

    chunks = near_recv_chunks = ns_sem.shape[0]
    chunk = pairs // chunks

    def near_copy(c):
        part = pl.ds(c * chunk, chunk)
        return pltpu.make_async_remote_copy(
            src_ref=near_send.at[part], dst_ref=near_recv.at[part],
            send_sem=ns_sem.at[c], recv_sem=nr_sem.at[c],
            device_id=(me, other), device_id_type=MESH,
        )

    for c in range(chunks):
        loop(chunk, lambda p: near_pair(c * chunk + p), 4)
        near_copy(c).start()

    def recv_roots(i, carry):
        root_recv(i).wait_recv()
        return carry

    lax.fori_loop(1, n, recv_roots, 0)
    half_n = n // 2
    uc[0] = jnp.zeros(uc.shape[1:], bf16)
    uc[1] = jnp.zeros(uc.shape[1:], bf16)
    loop(half_n, lambda j: uc.__setitem__(half_n + j, (roots[2 * j] + roots[2 * j + 1]).astype(bf16)), 4)
    size = half_n // 2
    while size >= 2:
        def upper_up(j):
            h = size + j
            x = mm(uc[2 * h], top_t[2 * h - 2]) + mm(uc[2 * h + 1], top_t[2 * h - 1])
            yield
            uc[h] = x.astype(bf16)

        loop(size, upper_up, 8)
        size //= 2
    terms = [mm(uc[ts[b]], top_c[b]) for b in range(top_blocks)]

    def upper_gather(j):
        h = j + 2
        total = None
        for b in range(top_blocks):
            term = terms[b] * (tt[b] == h).astype(f32)
            total = term if total is None else total + term
        g[h] = total

    loop(n - 2, upper_gather, 16)
    size = 2
    while size < half_n:
        def upper_down(j):
            h = size + j
            w = top_t[pl.ds(2 * h - 2, 2)].reshape(2 * width, width)
            x = mm_split(g[h], w, NT)
            even = g[2 * h] + x[:, :width]
            uneven = g[2 * h + 1] + x[:, width:]
            yield
            g[2 * h] = even
            g[2 * h + 1] = uneven

        loop(size, upper_down, 8)
        size *= 2

    def top_copy(i):
        peer = peer_of(i)
        return pltpu.make_async_remote_copy(
            src_ref=g.at[half_n + peer // 2], dst_ref=top_recv.at[me],
            send_sem=ts_sem.at[i], recv_sem=tr_sem.at[me],
            device_id=(peer, mine), device_id_type=MESH,
        )

    def top_wait(i):
        source = peer_of(i)
        return pltpu.make_async_remote_copy(
            src_ref=g.at[half_n + source // 2], dst_ref=top_recv.at[source],
            send_sem=ts_sem.at[i], recv_sem=tr_sem.at[source],
            device_id=(source, mine), device_id_type=MESH,
        )

    def send_top(i, carry):
        top_copy(i).start()
        return carry

    lax.fori_loop(1, n, send_top, 0)

    for part in range(2):
        @pl.when(has_left)
        def _():
            halo_send(0, part).wait_recv()

        @pl.when(has_right)
        def _():
            halo_send(1, part).wait_recv()

    for first, count, pair in layout:
        for place in range(2):
            base = 3 * first + 2 * place * count
            if count > 1:
                def unpack(p):
                    x = halo[place, pair + p]
                    cl[base + 2 * p] = x[:, :width]
                    cl[base + 2 * p + 1] = x[:, width:]

                loop(count // 2, unpack, 16)
            else:
                cl[base] = halo[place, pair][:, :width]

    depth = slots // 2 * width
    left_half = lax.broadcasted_iota(jnp.int32, (rows, 2 * width), 1) < width
    for first, count, pair in layout:
        base = 3 * first - (me - 1) * count

        def node_terms(t):
            c = [cl[jnp.clip(base + cs[k, first + t], 0, cl.shape[0] - 1)] for k in range(slots)]
            per = slots // 2
            x = jnp.concatenate(
                [jnp.concatenate(c[:per], axis=1), jnp.concatenate(c[per:], axis=1)], axis=0
            )
            w = coup[pl.ds(pl.multiple_of((first + t) * depth, depth), depth), :].astype(bf16)
            r = mm(x, w)
            return r[:rows], r[rows:]

        if count > 1:
            def pair_field(p):
                a0, b0 = node_terms(2 * p)
                a1, b1 = node_terms(2 * p + 1)
                even = a0 + pltpu.roll(b0, width, 1)
                uneven = pltpu.roll(a1, width, 1) + b1
                field[pair + p] = jnp.where(left_half, even, uneven)

            loop(count // 2, pair_field, 8)
        else:
            a0, b0 = node_terms(0)
            root_field = (a0 + pltpu.roll(b0, width, 1))[:, :width]

    def recv_top(i, total):
        top_wait(i).wait_recv()
        return total + top_recv[peer_of(i)]

    parent = lax.fori_loop(1, n, recv_top, g[half_n + me // 2])
    root_down = (root_field + mm_split(parent, trans[root_row], NT)).astype(bf16)

    def step_down(height, q, x):
        first, count, pair = layout[height]
        w = trans[pl.ds(first + 2 * q, 2)].reshape(2 * width, width)
        return (field[pair + q] + mm(x, w, NT)).astype(bf16)

    top_height = len(layout) - 2
    down[layout[top_height][2]] = step_down(top_height, 0, root_down)
    for height in range(top_height - 1, 0, -1):
        pair = layout[height][2]
        above = layout[height + 1][2]

        def descend(p):
            x = down[above + p]
            even = step_down(height, 2 * p, x[:, :width])
            uneven = step_down(height, 2 * p + 1, x[:, width:])
            yield
            down[pair + 2 * p] = even
            down[pair + 2 * p + 1] = uneven

        loop(layout[height][1] // 4, descend, 8)

    for c in range(chunks):
        near_copy(c).wait_recv()
    above = layout[1][2]

    def leaf_pair(p, x):
        y = step_down(0, p, x)
        far = jnp.concatenate(
            [mm(y[:, :width], basis[2 * p], NT), mm(y[:, width:], basis[2 * p + 1], NT)], axis=1
        )
        total = far + (near_own[p] + near_recv[p].astype(f32))
        out[:, pl.ds(pl.multiple_of(p * 2 * width, 2 * width), 2 * width)] = total.astype(bf16)

    def leaf_down(p):
        x = down[above + p]
        leaf_pair(2 * p, x[:, :width])
        leaf_pair(2 * p + 1, x[:, width:])

    loop(pairs // 2, leaf_down, 8)

    vec_send(0, 1).wait_send()
    vec_send(1, 0).wait_send()
    vec_send(1, 1).wait_send()

    @pl.when(has_far)
    def _():
        vec_send(2, 0).wait_send()
        vec_send(2, 1).wait_send()

    @pl.when(sends_right)
    def _():
        halo_send(0, 0).wait_send()
        halo_send(0, 1).wait_send()

    @pl.when(sends_left)
    def _():
        halo_send(1, 0).wait_send()
        halo_send(1, 1).wait_send()

    for c in range(chunks):
        near_copy(c).wait_send()

    def end_sends(i, carry):
        root_copy(i).wait_send()
        top_copy(i).wait_send()
        return carry

    lax.fori_loop(1, n, end_sends, 0)


def shards(
    vectors, leaf_basis, local_transfer, coupling, coupling_source,
    top_transfer, top_coupling, top_target, top_source, near_blocks, near_source,
):
    n = lax.axis_size("leaf")
    rows = vectors.shape[0]
    leaves, width, rank = leaf_basis.shape
    nodes = local_transfer.shape[0]
    slots = coupling.shape[1]
    pairs = leaves // 2
    pair_total = leaves
    chunks = 4
    any_spec = pl.BlockSpec(memory_space=pl.ANY)
    smem = pl.BlockSpec(memory_space=pltpu.SMEM)
    vmem = pl.BlockSpec(memory_space=pltpu.VMEM)
    dma = pltpu.SemaphoreType.DMA
    return pl.pallas_call(
        functools.partial(kernel, n),
        out_shape=jax.ShapeDtypeStruct(vectors.shape, bf16),
        in_specs=[any_spec] * 5 + [smem] * 4 + [vmem] * 2,
        out_specs=vmem,
        scratch_shapes=[
            pltpu.VMEM((3, 2) + vectors.shape, bf16),
            pltpu.VMEM((3 * leaves, 2 * rows, width), bf16),
            pltpu.VMEM(leaf_basis.shape, bf16),
            pltpu.VMEM((width, rank, nodes), bf16),
            pltpu.VMEM((slots, rank, rank, nodes), bf16),
            pltpu.VMEM(near_blocks.shape, bf16),
            pltpu.VMEM((nodes * rank // 2, 2 * rank), f32),
            pltpu.VMEM(local_transfer.shape, bf16),
            pltpu.VMEM((nodes * slots // 2 * rank, 2 * rank), f32),
            pltpu.VMEM((pair_total, rows, 2 * rank), bf16),
            pltpu.VMEM((2, pair_total, rows, 2 * rank), bf16),
            pltpu.VMEM((3 * nodes, rows, rank), bf16),
            pltpu.VMEM((pair_total, rows, 2 * rank), f32),
            pltpu.VMEM((pair_total, rows, 2 * rank), bf16),
            pltpu.VMEM((pairs, rows, 2 * width), f32),
            pltpu.VMEM((pairs, rows, 2 * width), bf16),
            pltpu.VMEM((pairs, rows, 2 * width), bf16),
            pltpu.VMEM((n, rows, rank), f32),
            pltpu.VMEM((n, rows, rank), bf16),
            pltpu.VMEM((n, rows, rank), f32),
            pltpu.VMEM((n, rows, rank), f32),
            dma((5,)),
            dma((3, 2)), dma((3, 2)),
            dma((2, 2)), dma((2, 2)),
            dma((chunks,)), dma((chunks,)),
            dma((n,)), dma((n,)),
            dma((n,)), dma((n,)),
        ],
        compiler_params=pltpu.CompilerParams(
            collective_id=0, has_side_effects=True, vmem_limit_bytes=56 * 1024 * 1024
        ),
    )(
        vectors, leaf_basis, local_transfer.transpose(1, 2, 0), coupling.transpose(1, 2, 3, 0), near_blocks,
        coupling_source.T, near_source.T, top_target, top_source, top_transfer, top_coupling,
    )


def solution(mesh):
    placed = (
        P("rhs", "leaf"),
        P("leaf", None, None),
        P("leaf", None, None),
        P("leaf", None, None, None),
        P("leaf", None),
        P(),
        P("leaf", None, None),
        P("leaf"),
        P("leaf"),
        P("leaf", "rhs", None, None),
        P("leaf", "rhs"),
    )
    return jax.shard_map(
        shards, mesh=mesh, in_specs=placed, out_specs=P("rhs", "leaf"), check_vma=False
    )
```

```python
import functools

import jax
import jax.numpy as jnp
from jax import lax
from jax.experimental import pallas as pl
from jax.experimental.pallas import tpu as pltpu
from jax.sharding import PartitionSpec as P

MESH = pl.DeviceIdType.MESH
NT = (((1,), (1,)), ((), ()))
NN = (((1,), (0,)), ((), ()))
f32 = jnp.float32
bf16 = jnp.bfloat16


def mm(a, b, dims=NN):
    return lax.dot_general(a, b, dims, preferred_element_type=f32)


def mm_split(a, b, dims):
    high = a.astype(bf16)
    low = (a - high.astype(f32)).astype(bf16)
    return mm(high, b, dims) + mm(low, b, dims)


def level_table(leaf_count):
    layout = []
    first, count, pair = 0, leaf_count, 0
    while count >= 1:
        layout.append((first, count, pair))
        first += count
        pair += max(count // 2, 1)
        count //= 2
    return layout


def loop(count, body, unroll):
    unroll = min(unroll, count)
    while count % unroll:
        unroll -= 1

    def step(i, carry):
        parts = [body(i * unroll + u) for u in range(unroll)]
        if hasattr(parts[0], "__next__"):
            for part in parts:
                next(part)
            for part in parts:
                next(part, None)
        return carry

    if count == unroll:
        step(0, 0)
    else:
        lax.fori_loop(0, count // unroll, step, 0)


def kernel(
    roots_n,
    vec, basis_h, trans_h, coup_h, near_h,
    cs, ns, tt, ts, top_t, top_c,
    out,
    vbuf, pts, basis, trans_raw, coup_raw, near, trans_rows, trans, coup,
    cp, halo, cl, field, down, near_own, near_send, near_recv,
    roots, uc, g, top_recv,
    local_sem, vs_sem, vr_sem, hs_sem, hr_sem, ns_sem, nr_sem, rs_sem, rr_sem, ts_sem, tr_sem,
):
    n = roots_n
    leaves = basis.shape[0]
    width = basis.shape[1]
    rows = vec.shape[0]
    layout = level_table(leaves)
    pairs = leaves // 2
    slots = coup_raw.shape[0]
    nodes = trans.shape[0]
    near_slots = near.shape[1]
    top_blocks = top_c.shape[0]
    me = lax.axis_index("leaf")
    mine = lax.axis_index("rhs")
    other = 1 - mine
    has_left, has_right = me > 0, me < n - 1
    odd = lax.rem(me, 2)
    buddy = me + 1 - 2 * odd
    far = me - 1 + 2 * odd
    has_far = jnp.logical_and(far >= 0, far < n)

    def peer_of(i):
        return lax.rem(me + i, n)

    barrier = pltpu.get_barrier_semaphore()

    def greet(i, carry):
        pl.semaphore_signal(barrier, inc=1, device_id=(peer_of(i), mine), device_id_type=MESH)
        return carry

    lax.fori_loop(1, n, greet, 0)
    pl.semaphore_signal(barrier, inc=1, device_id=(me, other), device_id_type=MESH)

    local = [
        pltpu.make_async_copy(src, dst, local_sem.at[i])
        for i, (src, dst) in enumerate(
            ((vec, vbuf.at[0, 0]), (basis_h, basis), (trans_h, trans_raw), (near_h, near), (coup_h, coup_raw))
        )
    ]
    for i in (0, 1, 2, 4):
        local[i].start()


    def vec_send(kind, half):
        source = vec
        if half == 1 and kind > 0:
            source = vbuf.at[0, 1] if kind == 1 else vbuf.at[2, 0]
        if kind == 1:
            target = (buddy, mine)
        elif kind == 2 and half == 0:
            target = (far, mine)
        else:
            target = (me, other)
        return pltpu.make_async_remote_copy(
            src_ref=source, dst_ref=vbuf.at[kind, half],
            send_sem=vs_sem.at[kind, half], recv_sem=vr_sem.at[kind, half],
            device_id=target, device_id_type=MESH,
        )

    def halo_send(place, part):
        part_pairs = pl.ds(0, pairs) if part == 0 else pl.ds(pairs, cp.shape[0] - pairs)
        return pltpu.make_async_remote_copy(
            src_ref=cp.at[part_pairs], dst_ref=halo.at[place, part_pairs],
            send_sem=hs_sem.at[place, part], recv_sem=hr_sem.at[place, part],
            device_id=(me + (1 - 2 * place), mine), device_id_type=MESH,
        )

    sends_right, sends_left = has_right, has_left
    local[0].wait()
    local[1].wait()

    def store_pair(pair_index, node_index, a, b):
        cp[pair_index] = jnp.concatenate([a, b], axis=1)
        cl[node_index] = a
        cl[node_index + 1] = b

    def turned(a, b):
        return jnp.concatenate([a, b], axis=0).T.astype(f32)

    def transfer_layout():
        half = width // 2
        pitch = half + 8

        def turn(m):
            trans_rows[pl.ds(m, nodes, stride=pitch), :] = turned(trans_raw[m], trans_raw[m + half])

        def split(t):
            x = trans_rows[pl.ds(pl.multiple_of(t * pitch, 8), half), :].astype(bf16)
            trans[t, :half, :] = x[:, :width]
            trans[t, half:, :] = x[:, width:]

        loop(half, turn, 8)
        whole = nodes // 16 * 16
        loop(whole, split, 16)
        for t in range(whole, nodes):
            split(t)

    def coupling_layout():
        per = slots // 2
        for k in range(per):
            def turn(m):
                coup[pl.ds(k * width + m, nodes, stride=per * width + 8), :] = turned(coup_raw[k, m], coup_raw[k + per, m])

            loop(width, turn, 8)

    def leaf_up(p):
        x = vbuf[0, 0, :, pl.ds(pl.multiple_of(p * 2 * width, 2 * width), 2 * width)]
        x0, x1 = x[:, :width], x[:, width:]
        c0 = mm(x0, basis[2 * p]).astype(bf16)
        c1 = mm(x1, basis[2 * p + 1]).astype(bf16)
        store_pair(p, leaves + 2 * p, c0, c1)

    loop(pairs, leaf_up, 16)
    local[3].start()
    pl.semaphore_wait(barrier, n)
    vec_send(0, 1).start()
    vec_send(1, 0).start()

    @pl.when(has_far)
    def _():
        vec_send(2, 0).start()


    @pl.when(sends_right)
    def _():
        halo_send(0, 0).start()

    @pl.when(sends_left)
    def _():
        halo_send(1, 0).start()

    local[2].wait()
    transfer_layout()
    for height in range(1, len(layout)):
        below_first, below_count, below_pair = layout[height - 1]
        first, count, pair = layout[height]

        def lift(q):
            w = trans[pl.ds(below_first + 2 * q, 2)].reshape(2 * width, width)
            return mm(cp[below_pair + q], w).astype(bf16)

        if count > 1:
            def up(p):
                a, b = lift(2 * p), lift(2 * p + 1)
                yield
                store_pair(pair + p, 3 * first + count + 2 * p, a, b)

            loop(count // 2, up, 16)
        else:
            c = lift(0)
            cp[pair] = jnp.concatenate([c, c], axis=1)
            cl[3 * first + count] = c
    root_row = layout[-1][0]
    root_pair = layout[-1][2]
    root_term = mm(cp[root_pair][:, :width], trans[root_row])
    roots[me] = root_term

    def root_copy(i):
        return pltpu.make_async_remote_copy(
            src_ref=roots.at[me], dst_ref=roots.at[me], send_sem=rs_sem, recv_sem=rr_sem,
            device_id=(peer_of(i), mine), device_id_type=MESH,
        )

    def all_peers(buffer, send_sem, recv_sem):
        part = buffer.at[pl.ds(0, n - 1)]
        return pltpu.make_async_remote_copy(
            src_ref=part, dst_ref=part, send_sem=send_sem, recv_sem=recv_sem,
            device_id=(peer_of(1), mine), device_id_type=MESH,
        )

    def send_roots(i, carry):
        root_copy(i).start()
        return carry

    lax.fori_loop(1, n, send_roots, 0)

    @pl.when(sends_right)
    def _():
        halo_send(0, 1).start()

    @pl.when(sends_left)
    def _():
        halo_send(1, 1).start()

    vec_send(0, 1).wait_recv()
    vec_send(1, 1).start()

    @pl.when(has_far)
    def _():
        vec_send(2, 0).wait_recv()
        vec_send(2, 1).start()

    local[4].wait()
    coupling_layout()

    def unpack_points(kind, half):
        place = (1, 2 - 2 * odd, 2 * odd)[kind]

        def body(p):
            x = vbuf[kind, half, :, pl.ds(pl.multiple_of(p * 2 * width, 2 * width), 2 * width)]
            pts[place * leaves + 2 * p, half * rows:(half + 1) * rows, :] = x[:, :width]
            pts[place * leaves + 2 * p + 1, half * rows:(half + 1) * rows, :] = x[:, width:]

        loop(pairs, body, 16)

    @pl.when(jnp.logical_not(has_far))
    def _():
        vbuf[2] = jnp.zeros(vbuf.shape[1:], bf16)

    @pl.when(jnp.logical_not(has_left))
    def _():
        halo[0] = jnp.zeros(halo.shape[1:], bf16)

    @pl.when(jnp.logical_not(has_right))
    def _():
        halo[1] = jnp.zeros(halo.shape[1:], bf16)

    unpack_points(0, 0)
    unpack_points(0, 1)
    vec_send(1, 0).wait_recv()
    unpack_points(1, 0)
    unpack_points(2, 0)
    vec_send(1, 1).wait_recv()
    unpack_points(1, 1)

    @pl.when(has_far)
    def _():
        vec_send(2, 1).wait_recv()

    unpack_points(2, 1)
    local[3].wait()
    leaf_base = (me - 1) * leaves

    def near_leaf(i):
        x = [pts[jnp.clip(ns[j, i] - leaf_base, 0, 3 * leaves - 1)] for j in range(near_slots)]
        blocks = [near[i, j] for j in range(near_slots)]
        return mm(jnp.concatenate(x, axis=1), jnp.concatenate(blocks, axis=1), NT)

    def near_pair(p):
        both = jnp.concatenate([near_leaf(2 * p), near_leaf(2 * p + 1)], axis=1)
        near_own[p] = both[:rows]
        near_send[p] = both[rows:].astype(bf16)

    chunks = near_recv_chunks = ns_sem.shape[0]
    chunk = pairs // chunks

    def near_copy(c):
        part = pl.ds(c * chunk, chunk)
        return pltpu.make_async_remote_copy(
            src_ref=near_send.at[part], dst_ref=near_recv.at[part],
            send_sem=ns_sem.at[c], recv_sem=nr_sem.at[c],
            device_id=(me, other), device_id_type=MESH,
        )

    for c in range(chunks):
        loop(chunk, lambda p: near_pair(c * chunk + p), 4)
        near_copy(c).start()

    all_peers(roots, rs_sem, rr_sem).wait_recv()
    half_n = n // 2
    uc[0] = jnp.zeros(uc.shape[1:], bf16)
    uc[1] = jnp.zeros(uc.shape[1:], bf16)
    loop(half_n, lambda j: uc.__setitem__(half_n + j, (roots[2 * j] + roots[2 * j + 1]).astype(bf16)), 4)
    size = half_n // 2
    while size >= 2:
        def upper_up(j):
            h = size + j
            x = mm(uc[2 * h], top_t[2 * h - 2]) + mm(uc[2 * h + 1], top_t[2 * h - 1])
            yield
            uc[h] = x.astype(bf16)

        loop(size, upper_up, 8)
        size //= 2
    terms = [mm(uc[ts[b]], top_c[b]) for b in range(top_blocks)]

    def upper_gather(j):
        h = j + 2
        total = None
        for b in range(top_blocks):
            term = terms[b] * (tt[b] == h).astype(f32)
            total = term if total is None else total + term
        g[h] = total

    loop(n - 2, upper_gather, 16)
    size = 2
    while size < half_n:
        def upper_down(j):
            h = size + j
            w = top_t[pl.ds(2 * h - 2, 2)].reshape(2 * width, width)
            x = mm_split(g[h], w, NT)
            even = g[2 * h] + x[:, :width]
            uneven = g[2 * h + 1] + x[:, width:]
            yield
            g[2 * h] = even
            g[2 * h + 1] = uneven

        loop(size, upper_down, 8)
        size *= 2

    top_recv[me] = g[half_n + me // 2]

    def top_copy(i):
        peer = peer_of(i)
        return pltpu.make_async_remote_copy(
            src_ref=g.at[half_n + peer // 2], dst_ref=top_recv.at[me], send_sem=ts_sem, recv_sem=tr_sem,
            device_id=(peer, mine), device_id_type=MESH,
        )

    def send_top(i, carry):
        top_copy(i).start()
        return carry

    lax.fori_loop(1, n, send_top, 0)

    for part in range(2):
        @pl.when(has_left)
        def _():
            halo_send(0, part).wait_recv()

        @pl.when(has_right)
        def _():
            halo_send(1, part).wait_recv()

    for first, count, pair in layout:
        for place in range(2):
            base = 3 * first + 2 * place * count
            if count > 1:
                def unpack(p):
                    x = halo[place, pair + p]
                    cl[base + 2 * p] = x[:, :width]
                    cl[base + 2 * p + 1] = x[:, width:]

                loop(count // 2, unpack, 16)
            else:
                cl[base] = halo[place, pair][:, :width]

    depth = slots // 2 * width
    left_half = lax.broadcasted_iota(jnp.int32, (rows, 2 * width), 1) < width
    for first, count, pair in layout:
        base = 3 * first - (me - 1) * count

        def node_terms(t):
            c = [cl[jnp.clip(base + cs[k, first + t], 0, cl.shape[0] - 1)] for k in range(slots)]
            per = slots // 2
            x = jnp.concatenate(
                [jnp.concatenate(c[:per], axis=1), jnp.concatenate(c[per:], axis=1)], axis=0
            )
            w = coup[pl.ds(pl.multiple_of((first + t) * (depth + 8), 8), depth), :].astype(bf16)
            r = mm(x, w)
            return r[:rows], r[rows:]

        if count > 1:
            def pair_field(p):
                a0, b0 = node_terms(2 * p)
                a1, b1 = node_terms(2 * p + 1)
                even = a0 + pltpu.roll(b0, width, 1)
                uneven = pltpu.roll(a1, width, 1) + b1
                field[pair + p] = jnp.where(left_half, even, uneven)

            loop(count // 2, pair_field, 8)
        else:
            a0, b0 = node_terms(0)
            root_field = (a0 + pltpu.roll(b0, width, 1))[:, :width]

    all_peers(top_recv, ts_sem, tr_sem).wait_recv()
    parent = top_recv[0]
    for i in range(1, n):
        parent = parent + top_recv[i]
    root_down = (root_field + mm_split(parent, trans[root_row], NT)).astype(bf16)

    def step_down(height, q, x):
        first, count, pair = layout[height]
        w = trans[pl.ds(first + 2 * q, 2)].reshape(2 * width, width)
        return (field[pair + q] + mm(x, w, NT)).astype(bf16)

    top_height = len(layout) - 2
    down[layout[top_height][2]] = step_down(top_height, 0, root_down)
    for height in range(top_height - 1, 0, -1):
        pair = layout[height][2]
        above = layout[height + 1][2]

        def descend(p):
            x = down[above + p]
            even = step_down(height, 2 * p, x[:, :width])
            uneven = step_down(height, 2 * p + 1, x[:, width:])
            yield
            down[pair + 2 * p] = even
            down[pair + 2 * p + 1] = uneven

        loop(layout[height][1] // 4, descend, 8)

    for c in range(chunks):
        near_copy(c).wait_recv()
    above = layout[1][2]

    def leaf_pair(p, x):
        y = step_down(0, p, x)
        far = jnp.concatenate(
            [mm(y[:, :width], basis[2 * p], NT), mm(y[:, width:], basis[2 * p + 1], NT)], axis=1
        )
        total = far + (near_own[p] + near_recv[p].astype(f32))
        out[:, pl.ds(pl.multiple_of(p * 2 * width, 2 * width), 2 * width)] = total.astype(bf16)

    def leaf_down(p):
        x = down[above + p]
        leaf_pair(2 * p, x[:, :width])
        leaf_pair(2 * p + 1, x[:, width:])

    loop(pairs // 2, leaf_down, 8)

    vec_send(0, 1).wait_send()
    vec_send(1, 0).wait_send()
    vec_send(1, 1).wait_send()

    @pl.when(has_far)
    def _():
        vec_send(2, 0).wait_send()
        vec_send(2, 1).wait_send()

    @pl.when(sends_right)
    def _():
        halo_send(0, 0).wait_send()
        halo_send(0, 1).wait_send()

    @pl.when(sends_left)
    def _():
        halo_send(1, 0).wait_send()
        halo_send(1, 1).wait_send()

    for c in range(chunks):
        near_copy(c).wait_send()

    all_peers(roots, rs_sem, rr_sem).wait_send()
    all_peers(top_recv, ts_sem, tr_sem).wait_send()


def shards(
    vectors, leaf_basis, local_transfer, coupling, coupling_source,
    top_transfer, top_coupling, top_target, top_source, near_blocks, near_source,
):
    n = lax.axis_size("leaf")
    rows = vectors.shape[0]
    leaves, width, rank = leaf_basis.shape
    nodes = local_transfer.shape[0]
    slots = coupling.shape[1]
    pairs = leaves // 2
    pair_total = leaves
    chunks = 4
    any_spec = pl.BlockSpec(memory_space=pl.ANY)
    smem = pl.BlockSpec(memory_space=pltpu.SMEM)
    vmem = pl.BlockSpec(memory_space=pltpu.VMEM)
    dma = pltpu.SemaphoreType.DMA
    return pl.pallas_call(
        functools.partial(kernel, n),
        out_shape=jax.ShapeDtypeStruct(vectors.shape, bf16),
        in_specs=[any_spec] * 5 + [smem] * 4 + [vmem] * 2,
        out_specs=vmem,
        scratch_shapes=[
            pltpu.VMEM((3, 2) + vectors.shape, bf16),
            pltpu.VMEM((3 * leaves, 2 * rows, width), bf16),
            pltpu.VMEM(leaf_basis.shape, bf16),
            pltpu.VMEM((width, rank, nodes), bf16),
            pltpu.VMEM((slots, rank, rank, nodes), bf16),
            pltpu.VMEM(near_blocks.shape, bf16),
            pltpu.VMEM((nodes * (rank // 2 + 8), 2 * rank), f32),
            pltpu.VMEM(local_transfer.shape, bf16),
            pltpu.VMEM((nodes * (slots // 2 * rank + 8), 2 * rank), f32),
            pltpu.VMEM((pair_total, rows, 2 * rank), bf16),
            pltpu.VMEM((2, pair_total, rows, 2 * rank), bf16),
            pltpu.VMEM((3 * nodes, rows, rank), bf16),
            pltpu.VMEM((pair_total, rows, 2 * rank), f32),
            pltpu.VMEM((pair_total, rows, 2 * rank), bf16),
            pltpu.VMEM((pairs, rows, 2 * width), f32),
            pltpu.VMEM((pairs, rows, 2 * width), bf16),
            pltpu.VMEM((pairs, rows, 2 * width), bf16),
            pltpu.VMEM((n, rows, rank), f32),
            pltpu.VMEM((n, rows, rank), bf16),
            pltpu.VMEM((n, rows, rank), f32),
            pltpu.VMEM((n, rows, rank), f32),
            dma((5,)),
            dma((3, 2)), dma((3, 2)),
            dma((2, 2)), dma((2, 2)),
            dma((chunks,)), dma((chunks,)),
            dma, dma, dma, dma,
        ],
        compiler_params=pltpu.CompilerParams(
            collective_id=0, has_side_effects=True, vmem_limit_bytes=56 * 1024 * 1024
        ),
    )(
        vectors, leaf_basis, local_transfer.transpose(1, 2, 0), coupling.transpose(1, 2, 3, 0), near_blocks,
        coupling_source.T, near_source.T, top_target, top_source, top_transfer, top_coupling,
    )


def solution(mesh):
    placed = (
        P("rhs", "leaf"),
        P("leaf", None, None),
        P("leaf", None, None),
        P("leaf", None, None, None),
        P("leaf", None),
        P(),
        P("leaf", None, None),
        P("leaf"),
        P("leaf"),
        P("leaf", "rhs", None, None),
        P("leaf", "rhs"),
    )
    return jax.shard_map(
        shards, mesh=mesh, in_specs=placed, out_specs=P("rhs", "leaf"), check_vma=False
    )
```

```python
import functools

import jax
import jax.numpy as jnp
from jax import lax
from jax.experimental import pallas as pl
from jax.experimental.pallas import tpu as pltpu
from jax.sharding import PartitionSpec as P

MESH = pl.DeviceIdType.MESH
NT = (((1,), (1,)), ((), ()))
NN = (((1,), (0,)), ((), ()))
f32 = jnp.float32
bf16 = jnp.bfloat16


def mm(a, b, dims=NN):
    return lax.dot_general(a, b, dims, preferred_element_type=f32)


def mm_split(a, b, dims):
    high = a.astype(bf16)
    low = (a - high.astype(f32)).astype(bf16)
    return mm(high, b, dims) + mm(low, b, dims)


def level_table(leaf_count):
    layout = []
    first, count, pair = 0, leaf_count, 0
    while count >= 1:
        layout.append((first, count, pair))
        first += count
        pair += max(count // 2, 1)
        count //= 2
    return layout


def loop(count, body, unroll):
    unroll = min(unroll, count)
    while count % unroll:
        unroll -= 1

    def step(i, carry):
        parts = [body(i * unroll + u) for u in range(unroll)]
        if hasattr(parts[0], "__next__"):
            for part in parts:
                next(part)
            for part in parts:
                next(part, None)
        return carry

    if count == unroll:
        step(0, 0)
    else:
        lax.fori_loop(0, count // unroll, step, 0)


def kernel(
    roots_n,
    vec, basis_h, trans_h, coup_h, near_h,
    cs, ns, tt, ts, top_t, top_c,
    out,
    vbuf, pts, basis, trans_raw, coup_raw, near, trans_rows, trans, coup,
    cp, halo, cl, field, down, near_own, near_send, near_recv,
    roots, uc, g, top_recv,
    local_sem, vs_sem, vr_sem, hs_sem, hr_sem, ns_sem, nr_sem, rs_sem, rr_sem, ts_sem, tr_sem,
):
    n = roots_n
    leaves = basis.shape[0]
    width = basis.shape[1]
    rows = vec.shape[0]
    layout = level_table(leaves)
    pairs = leaves // 2
    slots = coup_raw.shape[0]
    nodes = trans.shape[0]
    near_slots = near.shape[1]
    top_blocks = top_c.shape[0]
    me = lax.axis_index("leaf")
    mine = lax.axis_index("rhs")
    other = 1 - mine
    has_left, has_right = me > 0, me < n - 1
    odd = lax.rem(me, 2)
    buddy = me + 1 - 2 * odd
    far = me - 1 + 2 * odd
    has_far = jnp.logical_and(far >= 0, far < n)

    def peer_of(i):
        return lax.rem(me + i, n)

    barrier = pltpu.get_barrier_semaphore()

    def greet(i, carry):
        pl.semaphore_signal(barrier, inc=1, device_id=(peer_of(i), mine), device_id_type=MESH)
        return carry

    lax.fori_loop(1, n, greet, 0)
    pl.semaphore_signal(barrier, inc=1, device_id=(me, other), device_id_type=MESH)

    local = [
        pltpu.make_async_copy(src, dst, local_sem.at[i])
        for i, (src, dst) in enumerate(
            ((vec, vbuf.at[0, 0]), (basis_h, basis), (trans_h, trans_raw), (near_h, near), (coup_h, coup_raw))
        )
    ]
    for i in (0, 1, 2):
        local[i].start()


    def vec_send(kind, half):
        source = vec
        if half == 1 and kind > 0:
            source = vbuf.at[0, 1] if kind == 1 else vbuf.at[2, 0]
        if kind == 1:
            target = (buddy, mine)
        elif kind == 2 and half == 0:
            target = (far, mine)
        else:
            target = (me, other)
        return pltpu.make_async_remote_copy(
            src_ref=source, dst_ref=vbuf.at[kind, half],
            send_sem=vs_sem.at[kind, half], recv_sem=vr_sem.at[kind, half],
            device_id=target, device_id_type=MESH,
        )

    def halo_send(place, part):
        part_pairs = pl.ds(0, pairs) if part == 0 else pl.ds(pairs, cp.shape[0] - pairs)
        return pltpu.make_async_remote_copy(
            src_ref=cp.at[part_pairs], dst_ref=halo.at[place, part_pairs],
            send_sem=hs_sem.at[place, part], recv_sem=hr_sem.at[place, part],
            device_id=(me + (1 - 2 * place), mine), device_id_type=MESH,
        )

    sends_right, sends_left = has_right, has_left
    local[0].wait()
    local[1].wait()
    local[4].start()

    def store_pair(pair_index, node_index, a, b):
        cp[pair_index] = jnp.concatenate([a, b], axis=1)
        cl[node_index] = a
        cl[node_index + 1] = b

    def turned(a, b):
        return jnp.concatenate([a, b], axis=0).T.astype(f32)

    def transfer_layout():
        half = width // 2
        pitch = half + 8

        def turn(m):
            trans_rows[pl.ds(m, nodes, stride=pitch), :] = turned(trans_raw[m], trans_raw[m + half])

        def split(t):
            x = trans_rows[pl.ds(pl.multiple_of(t * pitch, 8), half), :].astype(bf16)
            trans[t, :half, :] = x[:, :width]
            trans[t, half:, :] = x[:, width:]

        loop(half, turn, 8)
        whole = nodes // 16 * 16
        loop(whole, split, 16)
        for t in range(whole, nodes):
            split(t)

    per = slots // 2

    def turn_coupling(k, m):
        coup[pl.ds(k * width + m, nodes, stride=per * width + 8), :] = turned(coup_raw[k, m], coup_raw[k + per, m])

    def leaf_up(p):
        x = vbuf[0, 0, :, pl.ds(pl.multiple_of(p * 2 * width, 2 * width), 2 * width)]
        x0, x1 = x[:, :width], x[:, width:]
        c0 = mm(x0, basis[2 * p]).astype(bf16)
        c1 = mm(x1, basis[2 * p + 1]).astype(bf16)
        store_pair(p, leaves + 2 * p, c0, c1)

    loop(pairs, leaf_up, 16)
    local[3].start()
    pl.semaphore_wait(barrier, n)
    vec_send(0, 1).start()
    vec_send(1, 0).start()

    @pl.when(has_far)
    def _():
        vec_send(2, 0).start()


    @pl.when(sends_right)
    def _():
        halo_send(0, 0).start()

    @pl.when(sends_left)
    def _():
        halo_send(1, 0).start()

    local[2].wait()
    transfer_layout()
    local[4].wait()
    early = 8
    for height in range(1, len(layout)):
        below_first, below_count, below_pair = layout[height - 1]
        first, count, pair = layout[height]

        def lift(q):
            w = trans[pl.ds(below_first + 2 * q, 2)].reshape(2 * width, width)
            return mm(cp[below_pair + q], w).astype(bf16)

        if count > 1:
            def up(p):
                a, b = lift(2 * p), lift(2 * p + 1)
                yield
                store_pair(pair + p, 3 * first + count + 2 * p, a, b)

            loop(count // 2, up, 16)
        else:
            c = lift(0)
            cp[pair] = jnp.concatenate([c, c], axis=1)
            cl[3 * first + count] = c
        for m in range(early * (height - 1), early * height):
            turn_coupling(0, m)
    root_row = layout[-1][0]
    root_pair = layout[-1][2]
    root_term = mm(cp[root_pair][:, :width], trans[root_row])
    roots[me] = root_term

    def root_copy(i):
        return pltpu.make_async_remote_copy(
            src_ref=roots.at[me], dst_ref=roots.at[me], send_sem=rs_sem, recv_sem=rr_sem,
            device_id=(peer_of(i), mine), device_id_type=MESH,
        )

    def all_peers(buffer, send_sem, recv_sem):
        part = buffer.at[pl.ds(0, n - 1)]
        return pltpu.make_async_remote_copy(
            src_ref=part, dst_ref=part, send_sem=send_sem, recv_sem=recv_sem,
            device_id=(peer_of(1), mine), device_id_type=MESH,
        )

    def send_roots(i, carry):
        root_copy(i).start()
        return carry

    lax.fori_loop(1, n, send_roots, 0)

    @pl.when(sends_right)
    def _():
        halo_send(0, 1).start()

    @pl.when(sends_left)
    def _():
        halo_send(1, 1).start()

    vec_send(0, 1).wait_recv()
    vec_send(1, 1).start()

    @pl.when(has_far)
    def _():
        vec_send(2, 0).wait_recv()
        vec_send(2, 1).start()

    turns_done = early * (len(layout) - 1)
    loop(width - turns_done, lambda m: turn_coupling(0, turns_done + m), 8)
    for k in range(1, per):
        loop(width, lambda m: turn_coupling(k, m), 8)

    def unpack_points(kind, half):
        place = (1, 2 - 2 * odd, 2 * odd)[kind]

        def body(p):
            x = vbuf[kind, half, :, pl.ds(pl.multiple_of(p * 2 * width, 2 * width), 2 * width)]
            pts[place * leaves + 2 * p, half * rows:(half + 1) * rows, :] = x[:, :width]
            pts[place * leaves + 2 * p + 1, half * rows:(half + 1) * rows, :] = x[:, width:]

        loop(pairs, body, 16)

    @pl.when(jnp.logical_not(has_far))
    def _():
        vbuf[2] = jnp.zeros(vbuf.shape[1:], bf16)

    @pl.when(jnp.logical_not(has_left))
    def _():
        halo[0] = jnp.zeros(halo.shape[1:], bf16)

    @pl.when(jnp.logical_not(has_right))
    def _():
        halo[1] = jnp.zeros(halo.shape[1:], bf16)

    unpack_points(0, 0)
    unpack_points(0, 1)
    vec_send(1, 0).wait_recv()
    unpack_points(1, 0)
    unpack_points(2, 0)
    vec_send(1, 1).wait_recv()
    unpack_points(1, 1)

    @pl.when(has_far)
    def _():
        vec_send(2, 1).wait_recv()

    unpack_points(2, 1)
    local[3].wait()
    leaf_base = (me - 1) * leaves

    def near_leaf(i):
        x = [pts[jnp.clip(ns[j, i] - leaf_base, 0, 3 * leaves - 1)] for j in range(near_slots)]
        blocks = [near[i, j] for j in range(near_slots)]
        return mm(jnp.concatenate(x, axis=1), jnp.concatenate(blocks, axis=1), NT)

    def near_pair(p):
        both = jnp.concatenate([near_leaf(2 * p), near_leaf(2 * p + 1)], axis=1)
        near_own[p] = both[:rows]
        near_send[p] = both[rows:].astype(bf16)

    chunks = near_recv_chunks = ns_sem.shape[0]
    chunk = pairs // chunks

    def near_copy(c):
        part = pl.ds(c * chunk, chunk)
        return pltpu.make_async_remote_copy(
            src_ref=near_send.at[part], dst_ref=near_recv.at[part],
            send_sem=ns_sem.at[c], recv_sem=nr_sem.at[c],
            device_id=(me, other), device_id_type=MESH,
        )

    for c in range(chunks - 1):
        loop(chunk, lambda p: near_pair(c * chunk + p), 4)
        near_copy(c).start()

    rest = list(range((chunks - 1) * chunk, pairs))

    def near_rest(count):
        for p in rest[:count]:
            near_pair(p)
        del rest[:count]

    all_peers(roots, rs_sem, rr_sem).wait_recv()
    half_n = n // 2
    uc[0] = jnp.zeros(uc.shape[1:], bf16)
    uc[1] = jnp.zeros(uc.shape[1:], bf16)
    loop(half_n, lambda j: uc.__setitem__(half_n + j, (roots[2 * j] + roots[2 * j + 1]).astype(bf16)), 4)
    size = half_n // 2
    while size >= 2:
        def upper_up(j):
            h = size + j
            x = mm(uc[2 * h], top_t[2 * h - 2]) + mm(uc[2 * h + 1], top_t[2 * h - 1])
            yield
            uc[h] = x.astype(bf16)

        loop(size, upper_up, 8)
        near_rest(2)
        size //= 2
    terms = [mm(uc[ts[b]], top_c[b]) for b in range(top_blocks)]
    near_rest(2)

    def upper_gather(j):
        h = j + 2
        total = None
        for b in range(top_blocks):
            term = terms[b] * (tt[b] == h).astype(f32)
            total = term if total is None else total + term
        g[h] = total

    loop(n - 2, upper_gather, 16)
    size = 2
    while size < half_n:
        def upper_down(j):
            h = size + j
            w = top_t[pl.ds(2 * h - 2, 2)].reshape(2 * width, width)
            x = mm_split(g[h], w, NT)
            even = g[2 * h] + x[:, :width]
            uneven = g[2 * h + 1] + x[:, width:]
            yield
            g[2 * h] = even
            g[2 * h + 1] = uneven

        loop(size, upper_down, 8)
        near_rest(1)
        size *= 2

    near_rest(len(rest))
    near_copy(chunks - 1).start()
    top_recv[me] = g[half_n + me // 2]

    def top_copy(i):
        peer = peer_of(i)
        return pltpu.make_async_remote_copy(
            src_ref=g.at[half_n + peer // 2], dst_ref=top_recv.at[me], send_sem=ts_sem, recv_sem=tr_sem,
            device_id=(peer, mine), device_id_type=MESH,
        )

    def send_top(i, carry):
        top_copy(i).start()
        return carry

    lax.fori_loop(1, n, send_top, 0)

    for part in range(2):
        @pl.when(has_left)
        def _():
            halo_send(0, part).wait_recv()

        @pl.when(has_right)
        def _():
            halo_send(1, part).wait_recv()

    for first, count, pair in layout:
        for place in range(2):
            base = 3 * first + 2 * place * count
            if count > 1:
                def unpack(p):
                    x = halo[place, pair + p]
                    cl[base + 2 * p] = x[:, :width]
                    cl[base + 2 * p + 1] = x[:, width:]

                loop(count // 2, unpack, 16)
            else:
                cl[base] = halo[place, pair][:, :width]

    depth = slots // 2 * width
    left_half = lax.broadcasted_iota(jnp.int32, (rows, 2 * width), 1) < width

    def node_terms(height, t):
        first, count, _ = layout[height]
        base = 3 * first - (me - 1) * count
        c = [cl[jnp.clip(base + cs[k, first + t], 0, cl.shape[0] - 1)] for k in range(slots)]
        x = jnp.concatenate(
            [jnp.concatenate(c[:per], axis=1), jnp.concatenate(c[per:], axis=1)], axis=0
        )
        w = coup[pl.ds(pl.multiple_of((first + t) * (depth + 8), 8), depth), :].astype(bf16)
        r = mm(x, w)
        return r[:rows], r[rows:]

    def pair_field(height, p):
        a0, b0 = node_terms(height, 2 * p)
        a1, b1 = node_terms(height, 2 * p + 1)
        even = a0 + pltpu.roll(b0, width, 1)
        uneven = pltpu.roll(a1, width, 1) + b1
        field[layout[height][2] + p] = jnp.where(left_half, even, uneven)

    a0, b0 = node_terms(len(layout) - 1, 0)
    root_field = (a0 + pltpu.roll(b0, width, 1))[:, :width]
    for height in range(len(layout) - 2, 0, -1):
        loop(layout[height][1] // 2, lambda p: pair_field(height, p), 16)

    all_peers(top_recv, ts_sem, tr_sem).wait_recv()
    parent = top_recv[0]
    for i in range(1, n):
        parent = parent + top_recv[i]
    root_down = (root_field + mm_split(parent, trans[root_row], NT)).astype(bf16)

    def step_down(height, q, x):
        first, count, pair = layout[height]
        w = trans[pl.ds(first + 2 * q, 2)].reshape(2 * width, width)
        return (field[pair + q] + mm(x, w, NT)).astype(bf16)

    top_height = len(layout) - 2
    down[layout[top_height][2]] = step_down(top_height, 0, root_down)
    share = pairs // (len(layout) + 1)
    for height in range(top_height - 1, 0, -1):
        pair = layout[height][2]
        above = layout[height + 1][2]

        def descend(p):
            x = down[above + p]
            even = step_down(height, 2 * p, x[:, :width])
            uneven = step_down(height, 2 * p + 1, x[:, width:])
            yield
            down[pair + 2 * p] = even
            down[pair + 2 * p + 1] = uneven

        loop(layout[height][1] // 4, descend, 8)
        for p in range(share * (top_height - 1 - height), share * (top_height - height)):
            pair_field(0, p)
    fields_done = share * (top_height - 1)
    loop(pairs - fields_done, lambda p: pair_field(0, fields_done + p), 8)

    for c in range(chunks):
        near_copy(c).wait_recv()
    above = layout[1][2]

    def leaf_pair(p, x):
        y = step_down(0, p, x)
        far = jnp.concatenate(
            [mm(y[:, :width], basis[2 * p], NT), mm(y[:, width:], basis[2 * p + 1], NT)], axis=1
        )
        total = far + (near_own[p] + near_recv[p].astype(f32))
        out[:, pl.ds(pl.multiple_of(p * 2 * width, 2 * width), 2 * width)] = total.astype(bf16)

    def leaf_down(p):
        x = down[above + p]
        leaf_pair(2 * p, x[:, :width])
        leaf_pair(2 * p + 1, x[:, width:])

    loop(pairs // 2, leaf_down, 8)

    vec_send(0, 1).wait_send()
    vec_send(1, 0).wait_send()
    vec_send(1, 1).wait_send()

    @pl.when(has_far)
    def _():
        vec_send(2, 0).wait_send()
        vec_send(2, 1).wait_send()

    @pl.when(sends_right)
    def _():
        halo_send(0, 0).wait_send()
        halo_send(0, 1).wait_send()

    @pl.when(sends_left)
    def _():
        halo_send(1, 0).wait_send()
        halo_send(1, 1).wait_send()

    for c in range(chunks):
        near_copy(c).wait_send()

    all_peers(roots, rs_sem, rr_sem).wait_send()
    all_peers(top_recv, ts_sem, tr_sem).wait_send()


def shards(
    vectors, leaf_basis, local_transfer, coupling, coupling_source,
    top_transfer, top_coupling, top_target, top_source, near_blocks, near_source,
):
    n = lax.axis_size("leaf")
    rows = vectors.shape[0]
    leaves, width, rank = leaf_basis.shape
    nodes = local_transfer.shape[0]
    slots = coupling.shape[1]
    pairs = leaves // 2
    pair_total = leaves
    chunks = 4
    any_spec = pl.BlockSpec(memory_space=pl.ANY)
    smem = pl.BlockSpec(memory_space=pltpu.SMEM)
    vmem = pl.BlockSpec(memory_space=pltpu.VMEM)
    dma = pltpu.SemaphoreType.DMA
    return pl.pallas_call(
        functools.partial(kernel, n),
        out_shape=jax.ShapeDtypeStruct(vectors.shape, bf16),
        in_specs=[any_spec] * 5 + [smem] * 4 + [vmem] * 2,
        out_specs=vmem,
        scratch_shapes=[
            pltpu.VMEM((3, 2) + vectors.shape, bf16),
            pltpu.VMEM((3 * leaves, 2 * rows, width), bf16),
            pltpu.VMEM(leaf_basis.shape, bf16),
            pltpu.VMEM((width, rank, nodes), bf16),
            pltpu.VMEM((slots, rank, rank, nodes), bf16),
            pltpu.VMEM(near_blocks.shape, bf16),
            pltpu.VMEM((nodes * (rank // 2 + 8), 2 * rank), f32),
            pltpu.VMEM(local_transfer.shape, bf16),
            pltpu.VMEM((nodes * (slots // 2 * rank + 8), 2 * rank), f32),
            pltpu.VMEM((pair_total, rows, 2 * rank), bf16),
            pltpu.VMEM((2, pair_total, rows, 2 * rank), bf16),
            pltpu.VMEM((3 * nodes, rows, rank), bf16),
            pltpu.VMEM((pair_total, rows, 2 * rank), f32),
            pltpu.VMEM((pair_total, rows, 2 * rank), bf16),
            pltpu.VMEM((pairs, rows, 2 * width), f32),
            pltpu.VMEM((pairs, rows, 2 * width), bf16),
            pltpu.VMEM((pairs, rows, 2 * width), bf16),
            pltpu.VMEM((n, rows, rank), f32),
            pltpu.VMEM((n, rows, rank), bf16),
            pltpu.VMEM((n, rows, rank), f32),
            pltpu.VMEM((n, rows, rank), f32),
            dma((5,)),
            dma((3, 2)), dma((3, 2)),
            dma((2, 2)), dma((2, 2)),
            dma((chunks,)), dma((chunks,)),
            dma, dma, dma, dma,
        ],
        compiler_params=pltpu.CompilerParams(
            collective_id=0, has_side_effects=True, vmem_limit_bytes=56 * 1024 * 1024
        ),
    )(
        vectors, leaf_basis, local_transfer.transpose(1, 2, 0), coupling.transpose(1, 2, 3, 0), near_blocks,
        coupling_source.T, near_source.T, top_target, top_source, top_transfer, top_coupling,
    )


def solution(mesh):
    placed = (
        P("rhs", "leaf"),
        P("leaf", None, None),
        P("leaf", None, None),
        P("leaf", None, None, None),
        P("leaf", None),
        P(),
        P("leaf", None, None),
        P("leaf"),
        P("leaf"),
        P("leaf", "rhs", None, None),
        P("leaf", "rhs"),
    )
    return jax.shard_map(
        shards, mesh=mesh, in_specs=placed, out_specs=P("rhs", "leaf"), check_vma=False
    )
```

```python
import functools

import jax
import jax.numpy as jnp
from jax import lax
from jax.experimental import pallas as pl
from jax.experimental.pallas import tpu as pltpu
from jax.sharding import PartitionSpec as P

MESH = pl.DeviceIdType.MESH
NT = (((1,), (1,)), ((), ()))
NN = (((1,), (0,)), ((), ()))
f32 = jnp.float32
bf16 = jnp.bfloat16


def mm(a, b, dims=NN):
    return lax.dot_general(a, b, dims, preferred_element_type=f32)


def mm_split(a, b, dims):
    high = a.astype(bf16)
    low = (a - high.astype(f32)).astype(bf16)
    return mm(high, b, dims) + mm(low, b, dims)


def level_table(leaf_count):
    layout = []
    first, count, pair = 0, leaf_count, 0
    while count >= 1:
        layout.append((first, count, pair))
        first += count
        pair += max(count // 2, 1)
        count //= 2
    return layout


def loop(count, body, unroll):
    unroll = min(unroll, count)
    while count % unroll:
        unroll -= 1

    def step(i, carry):
        parts = [body(i * unroll + u) for u in range(unroll)]
        if hasattr(parts[0], "__next__"):
            for part in parts:
                next(part)
            for part in parts:
                next(part, None)
        return carry

    if count == unroll:
        step(0, 0)
    else:
        lax.fori_loop(0, count // unroll, step, 0)


def kernel(
    roots_n,
    vec, basis_h, trans_h, coup_h, near_h,
    cs, ns, tt, ts, top_t, top_c,
    out,
    vbuf, pts, basis, trans_raw, coup_raw, near, trans_rows, trans, coup,
    cp, halo, cl, field, down, near_own, near_send, near_recv,
    roots, uc, g, top_recv,
    local_sem, vs_sem, vr_sem, hs_sem, hr_sem, ns_sem, nr_sem, rs_sem, rr_sem, ts_sem, tr_sem,
):
    n = roots_n
    leaves = basis.shape[0]
    width = basis.shape[1]
    rows = vec.shape[0]
    layout = level_table(leaves)
    pairs = leaves // 2
    slots = coup_raw.shape[0]
    nodes = trans.shape[0]
    near_slots = near.shape[1]
    top_blocks = top_c.shape[0]
    me = lax.axis_index("leaf")
    mine = lax.axis_index("rhs")
    other = 1 - mine
    has_left, has_right = me > 0, me < n - 1
    odd = lax.rem(me, 2)
    buddy = me + 1 - 2 * odd
    far = me - 1 + 2 * odd
    has_far = jnp.logical_and(far >= 0, far < n)

    def peer_of(i):
        return lax.rem(me + i, n)

    barrier = pltpu.get_barrier_semaphore()

    def greet(i, carry):
        pl.semaphore_signal(barrier, inc=1, device_id=(peer_of(i), mine), device_id_type=MESH)
        return carry

    lax.fori_loop(1, n, greet, 0)
    pl.semaphore_signal(barrier, inc=1, device_id=(me, other), device_id_type=MESH)

    local = [
        pltpu.make_async_copy(src, dst, local_sem.at[i])
        for i, (src, dst) in enumerate(
            ((vec, vbuf.at[0, 0]), (basis_h, basis), (trans_h, trans_raw), (near_h, near), (coup_h, coup_raw))
        )
    ]
    for i in (0, 1, 2):
        local[i].start()


    def vec_send(kind, half):
        source = vec
        if half == 1 and kind > 0:
            source = vbuf.at[0, 1] if kind == 1 else vbuf.at[2, 0]
        if kind == 1:
            target = (buddy, mine)
        elif kind == 2 and half == 0:
            target = (far, mine)
        else:
            target = (me, other)
        return pltpu.make_async_remote_copy(
            src_ref=source, dst_ref=vbuf.at[kind, half],
            send_sem=vs_sem.at[kind, half], recv_sem=vr_sem.at[kind, half],
            device_id=target, device_id_type=MESH,
        )

    def halo_send(place, part):
        part_pairs = pl.ds(0, pairs) if part == 0 else pl.ds(pairs, cp.shape[0] - pairs)
        return pltpu.make_async_remote_copy(
            src_ref=cp.at[part_pairs], dst_ref=halo.at[place, part_pairs],
            send_sem=hs_sem.at[place, part], recv_sem=hr_sem.at[place, part],
            device_id=(me + (1 - 2 * place), mine), device_id_type=MESH,
        )

    sends_right, sends_left = has_right, has_left
    pl.semaphore_wait(barrier, n)

    @pl.when(has_far)
    def _():
        vec_send(2, 0).start()

    vec_send(0, 1).start()
    vec_send(1, 0).start()

    local[0].wait()
    local[1].wait()
    local[4].start()

    def store_pair(pair_index, node_index, a, b):
        cp[pair_index] = jnp.concatenate([a, b], axis=1)
        cl[node_index] = a
        cl[node_index + 1] = b

    def turned(a, b):
        return jnp.concatenate([a, b], axis=0).T.astype(f32)

    def transfer_layout():
        half = width // 2
        pitch = half + 8

        def turn(m):
            trans_rows[pl.ds(m, nodes, stride=pitch), :] = turned(trans_raw[m], trans_raw[m + half])

        def split(t):
            x = trans_rows[pl.ds(pl.multiple_of(t * pitch, 8), half), :].astype(bf16)
            trans[t, :half, :] = x[:, :width]
            trans[t, half:, :] = x[:, width:]

        loop(half, turn, 8)
        whole = nodes // 16 * 16
        loop(whole, split, 16)
        for t in range(whole, nodes):
            split(t)

    per = slots // 2

    def turn_coupling(k, m):
        coup[pl.ds(k * width + m, nodes, stride=per * width + 8), :] = turned(coup_raw[k, m], coup_raw[k + per, m])

    def leaf_up(p):
        x = vbuf[0, 0, :, pl.ds(pl.multiple_of(p * 2 * width, 2 * width), 2 * width)]
        x0, x1 = x[:, :width], x[:, width:]
        c0 = mm(x0, basis[2 * p]).astype(bf16)
        c1 = mm(x1, basis[2 * p + 1]).astype(bf16)
        store_pair(p, leaves + 2 * p, c0, c1)

    loop(pairs, leaf_up, 16)
    local[3].start()

    @pl.when(sends_right)
    def _():
        halo_send(0, 0).start()

    @pl.when(sends_left)
    def _():
        halo_send(1, 0).start()

    local[2].wait()
    transfer_layout()
    local[4].wait()
    early = 4
    for height in range(1, len(layout)):
        below_first, below_count, below_pair = layout[height - 1]
        first, count, pair = layout[height]

        def lift(q):
            w = trans[pl.ds(below_first + 2 * q, 2)].reshape(2 * width, width)
            return mm(cp[below_pair + q], w).astype(bf16)

        if count > 1:
            def up(p):
                a, b = lift(2 * p), lift(2 * p + 1)
                yield
                store_pair(pair + p, 3 * first + count + 2 * p, a, b)

            loop(count // 2, up, 16)
        else:
            c = lift(0)
            cp[pair] = jnp.concatenate([c, c], axis=1)
            cl[3 * first + count] = c
        for m in range(early * (height - 1), early * height):
            turn_coupling(0, m)
    root_row = layout[-1][0]
    root_pair = layout[-1][2]
    root_term = mm(cp[root_pair][:, :width], trans[root_row])
    roots[me] = root_term

    def root_copy(i):
        return pltpu.make_async_remote_copy(
            src_ref=roots.at[me], dst_ref=roots.at[me], send_sem=rs_sem, recv_sem=rr_sem,
            device_id=(peer_of(i), mine), device_id_type=MESH,
        )

    def all_peers(buffer, send_sem, recv_sem):
        part = buffer.at[pl.ds(0, n - 1)]
        return pltpu.make_async_remote_copy(
            src_ref=part, dst_ref=part, send_sem=send_sem, recv_sem=recv_sem,
            device_id=(peer_of(1), mine), device_id_type=MESH,
        )

    def send_roots(i, carry):
        root_copy(i).start()
        return carry

    lax.fori_loop(1, n, send_roots, 0)

    @pl.when(sends_right)
    def _():
        halo_send(0, 1).start()

    @pl.when(sends_left)
    def _():
        halo_send(1, 1).start()

    vec_send(0, 1).wait_recv()
    vec_send(1, 1).start()

    @pl.when(has_far)
    def _():
        vec_send(2, 0).wait_recv()
        vec_send(2, 1).start()

    turns_done = early * (len(layout) - 1)
    loop(width - turns_done, lambda m: turn_coupling(0, turns_done + m), 8)
    for k in range(1, per):
        loop(width, lambda m: turn_coupling(k, m), 8)

    def unpack_points(kind, half):
        place = (1, 2 - 2 * odd, 2 * odd)[kind]

        def body(p):
            x = vbuf[kind, half, :, pl.ds(pl.multiple_of(p * 2 * width, 2 * width), 2 * width)]
            pts[place * leaves + 2 * p, half * rows:(half + 1) * rows, :] = x[:, :width]
            pts[place * leaves + 2 * p + 1, half * rows:(half + 1) * rows, :] = x[:, width:]

        loop(pairs, body, 16)

    @pl.when(jnp.logical_not(has_far))
    def _():
        vbuf[2] = jnp.zeros(vbuf.shape[1:], bf16)

    @pl.when(jnp.logical_not(has_left))
    def _():
        halo[0] = jnp.zeros(halo.shape[1:], bf16)

    @pl.when(jnp.logical_not(has_right))
    def _():
        halo[1] = jnp.zeros(halo.shape[1:], bf16)

    unpack_points(0, 0)
    unpack_points(0, 1)
    vec_send(1, 0).wait_recv()
    unpack_points(1, 0)
    unpack_points(2, 0)
    vec_send(1, 1).wait_recv()
    unpack_points(1, 1)

    @pl.when(has_far)
    def _():
        vec_send(2, 1).wait_recv()

    unpack_points(2, 1)
    local[3].wait()
    leaf_base = (me - 1) * leaves

    def near_leaf(i):
        x = [pts[jnp.clip(ns[j, i] - leaf_base, 0, 3 * leaves - 1)] for j in range(near_slots)]
        blocks = [near[i, j] for j in range(near_slots)]
        return mm(jnp.concatenate(x, axis=1), jnp.concatenate(blocks, axis=1), NT)

    def near_pair(p):
        both = jnp.concatenate([near_leaf(2 * p), near_leaf(2 * p + 1)], axis=1)
        near_own[p] = both[:rows]
        near_send[p] = both[rows:].astype(bf16)

    chunks = near_recv_chunks = ns_sem.shape[0]
    chunk = pairs // chunks

    def near_copy(c):
        part = pl.ds(c * chunk, chunk)
        return pltpu.make_async_remote_copy(
            src_ref=near_send.at[part], dst_ref=near_recv.at[part],
            send_sem=ns_sem.at[c], recv_sem=nr_sem.at[c],
            device_id=(me, other), device_id_type=MESH,
        )

    for c in range(chunks - 1):
        loop(chunk, lambda p: near_pair(c * chunk + p), 4)
        near_copy(c).start()

    rest = list(range((chunks - 1) * chunk, pairs))

    def near_rest(count):
        for p in rest[:count]:
            near_pair(p)
        del rest[:count]

    all_peers(roots, rs_sem, rr_sem).wait_recv()
    half_n = n // 2
    uc[0] = jnp.zeros(uc.shape[1:], bf16)
    uc[1] = jnp.zeros(uc.shape[1:], bf16)
    loop(half_n, lambda j: uc.__setitem__(half_n + j, (roots[2 * j] + roots[2 * j + 1]).astype(bf16)), 4)
    size = half_n // 2
    while size >= 2:
        def upper_up(j):
            h = size + j
            x = mm(uc[2 * h], top_t[2 * h - 2]) + mm(uc[2 * h + 1], top_t[2 * h - 1])
            yield
            uc[h] = x.astype(bf16)

        loop(size, upper_up, 8)
        near_rest(2)
        size //= 2
    terms = [mm(uc[ts[b]], top_c[b]) for b in range(top_blocks)]
    near_rest(2)

    def upper_gather(j):
        h = j + 2
        total = None
        for b in range(top_blocks):
            term = terms[b] * (tt[b] == h).astype(f32)
            total = term if total is None else total + term
        g[h] = total

    loop(n - 2, upper_gather, 16)
    size = 2
    while size < half_n:
        def upper_down(j):
            h = size + j
            w = top_t[pl.ds(2 * h - 2, 2)].reshape(2 * width, width)
            x = mm_split(g[h], w, NT)
            even = g[2 * h] + x[:, :width]
            uneven = g[2 * h + 1] + x[:, width:]
            yield
            g[2 * h] = even
            g[2 * h + 1] = uneven

        loop(size, upper_down, 8)
        near_rest(1)
        size *= 2

    near_rest(len(rest))
    near_copy(chunks - 1).start()
    top_recv[me] = g[half_n + me // 2]

    def top_copy(i):
        peer = peer_of(i)
        return pltpu.make_async_remote_copy(
            src_ref=g.at[half_n + peer // 2], dst_ref=top_recv.at[me], send_sem=ts_sem, recv_sem=tr_sem,
            device_id=(peer, mine), device_id_type=MESH,
        )

    def send_top(i, carry):
        top_copy(i).start()
        return carry

    lax.fori_loop(1, n, send_top, 0)

    for part in range(2):
        @pl.when(has_left)
        def _():
            halo_send(0, part).wait_recv()

        @pl.when(has_right)
        def _():
            halo_send(1, part).wait_recv()

    for first, count, pair in layout:
        for place in range(2):
            base = 3 * first + 2 * place * count
            if count > 1:
                def unpack(p):
                    x = halo[place, pair + p]
                    cl[base + 2 * p] = x[:, :width]
                    cl[base + 2 * p + 1] = x[:, width:]

                loop(count // 2, unpack, 16)
            else:
                cl[base] = halo[place, pair][:, :width]

    depth = slots // 2 * width
    left_half = lax.broadcasted_iota(jnp.int32, (rows, 2 * width), 1) < width

    def node_terms(height, t):
        first, count, _ = layout[height]
        base = 3 * first - (me - 1) * count
        c = [cl[jnp.clip(base + cs[k, first + t], 0, cl.shape[0] - 1)] for k in range(slots)]
        x = jnp.concatenate(
            [jnp.concatenate(c[:per], axis=1), jnp.concatenate(c[per:], axis=1)], axis=0
        )
        w = coup[pl.ds(pl.multiple_of((first + t) * (depth + 8), 8), depth), :].astype(bf16)
        r = mm(x, w)
        return r[:rows], r[rows:]

    def pair_field(height, p):
        a0, b0 = node_terms(height, 2 * p)
        a1, b1 = node_terms(height, 2 * p + 1)
        even = a0 + pltpu.roll(b0, width, 1)
        uneven = pltpu.roll(a1, width, 1) + b1
        field[layout[height][2] + p] = jnp.where(left_half, even, uneven)

    a0, b0 = node_terms(len(layout) - 1, 0)
    root_field = (a0 + pltpu.roll(b0, width, 1))[:, :width]
    for height in range(len(layout) - 2, 0, -1):
        loop(layout[height][1] // 2, lambda p: pair_field(height, p), 16)

    all_peers(top_recv, ts_sem, tr_sem).wait_recv()
    parent = top_recv[0]
    for i in range(1, n):
        parent = parent + top_recv[i]
    root_down = (root_field + mm_split(parent, trans[root_row], NT)).astype(bf16)

    def step_down(height, q, x):
        first, count, pair = layout[height]
        w = trans[pl.ds(first + 2 * q, 2)].reshape(2 * width, width)
        return (field[pair + q] + mm(x, w, NT)).astype(bf16)

    top_height = len(layout) - 2
    down[layout[top_height][2]] = step_down(top_height, 0, root_down)
    share = pairs // (len(layout) + 1)
    for height in range(top_height - 1, 0, -1):
        pair = layout[height][2]
        above = layout[height + 1][2]

        def descend(p):
            x = down[above + p]
            even = step_down(height, 2 * p, x[:, :width])
            uneven = step_down(height, 2 * p + 1, x[:, width:])
            yield
            down[pair + 2 * p] = even
            down[pair + 2 * p + 1] = uneven

        loop(layout[height][1] // 4, descend, 8)
        for p in range(share * (top_height - 1 - height), share * (top_height - height)):
            pair_field(0, p)
    fields_done = share * (top_height - 1)
    loop(pairs - fields_done, lambda p: pair_field(0, fields_done + p), 8)

    for c in range(chunks):
        near_copy(c).wait_recv()
    above = layout[1][2]

    def leaf_pair(p, x):
        y = step_down(0, p, x)
        far = jnp.concatenate(
            [mm(y[:, :width], basis[2 * p], NT), mm(y[:, width:], basis[2 * p + 1], NT)], axis=1
        )
        total = far + (near_own[p] + near_recv[p].astype(f32))
        out[:, pl.ds(pl.multiple_of(p * 2 * width, 2 * width), 2 * width)] = total.astype(bf16)

    def leaf_down(p):
        x = down[above + p]
        leaf_pair(2 * p, x[:, :width])
        leaf_pair(2 * p + 1, x[:, width:])

    loop(pairs // 2, leaf_down, 8)

    vec_send(0, 1).wait_send()
    vec_send(1, 0).wait_send()
    vec_send(1, 1).wait_send()

    @pl.when(has_far)
    def _():
        vec_send(2, 0).wait_send()
        vec_send(2, 1).wait_send()

    @pl.when(sends_right)
    def _():
        halo_send(0, 0).wait_send()
        halo_send(0, 1).wait_send()

    @pl.when(sends_left)
    def _():
        halo_send(1, 0).wait_send()
        halo_send(1, 1).wait_send()

    for c in range(chunks):
        near_copy(c).wait_send()

    all_peers(roots, rs_sem, rr_sem).wait_send()
    all_peers(top_recv, ts_sem, tr_sem).wait_send()


def shards(
    vectors, leaf_basis, local_transfer, coupling, coupling_source,
    top_transfer, top_coupling, top_target, top_source, near_blocks, near_source,
):
    n = lax.axis_size("leaf")
    rows = vectors.shape[0]
    leaves, width, rank = leaf_basis.shape
    nodes = local_transfer.shape[0]
    slots = coupling.shape[1]
    pairs = leaves // 2
    pair_total = leaves
    chunks = 4
    any_spec = pl.BlockSpec(memory_space=pl.ANY)
    smem = pl.BlockSpec(memory_space=pltpu.SMEM)
    vmem = pl.BlockSpec(memory_space=pltpu.VMEM)
    dma = pltpu.SemaphoreType.DMA
    return pl.pallas_call(
        functools.partial(kernel, n),
        out_shape=jax.ShapeDtypeStruct(vectors.shape, bf16),
        in_specs=[any_spec] * 5 + [smem] * 4 + [vmem] * 2,
        out_specs=vmem,
        scratch_shapes=[
            pltpu.VMEM((3, 2) + vectors.shape, bf16),
            pltpu.VMEM((3 * leaves, 2 * rows, width), bf16),
            pltpu.VMEM(leaf_basis.shape, bf16),
            pltpu.VMEM((width, rank, nodes), bf16),
            pltpu.VMEM((slots, rank, rank, nodes), bf16),
            pltpu.VMEM(near_blocks.shape, bf16),
            pltpu.VMEM((nodes * (rank // 2 + 8), 2 * rank), f32),
            pltpu.VMEM(local_transfer.shape, bf16),
            pltpu.VMEM((nodes * (slots // 2 * rank + 8), 2 * rank), f32),
            pltpu.VMEM((pair_total, rows, 2 * rank), bf16),
            pltpu.VMEM((2, pair_total, rows, 2 * rank), bf16),
            pltpu.VMEM((3 * nodes, rows, rank), bf16),
            pltpu.VMEM((pair_total, rows, 2 * rank), f32),
            pltpu.VMEM((pair_total, rows, 2 * rank), bf16),
            pltpu.VMEM((pairs, rows, 2 * width), f32),
            pltpu.VMEM((pairs, rows, 2 * width), bf16),
            pltpu.VMEM((pairs, rows, 2 * width), bf16),
            pltpu.VMEM((n, rows, rank), f32),
            pltpu.VMEM((n, rows, rank), bf16),
            pltpu.VMEM((n, rows, rank), f32),
            pltpu.VMEM((n, rows, rank), f32),
            dma((5,)),
            dma((3, 2)), dma((3, 2)),
            dma((2, 2)), dma((2, 2)),
            dma((chunks,)), dma((chunks,)),
            dma, dma, dma, dma,
        ],
        compiler_params=pltpu.CompilerParams(
            collective_id=0, has_side_effects=True, vmem_limit_bytes=56 * 1024 * 1024
        ),
    )(
        vectors, leaf_basis, local_transfer.transpose(1, 2, 0), coupling.transpose(1, 2, 3, 0), near_blocks,
        coupling_source.T, near_source.T, top_target, top_source, top_transfer, top_coupling,
    )


def solution(mesh):
    placed = (
        P("rhs", "leaf"),
        P("leaf", None, None),
        P("leaf", None, None),
        P("leaf", None, None, None),
        P("leaf", None),
        P(),
        P("leaf", None, None),
        P("leaf"),
        P("leaf"),
        P("leaf", "rhs", None, None),
        P("leaf", "rhs"),
    )
    return jax.shard_map(
        shards, mesh=mesh, in_specs=placed, out_specs=P("rhs", "leaf"), check_vma=False
    )
```

```python
import functools

import jax
import jax.numpy as jnp
from jax import lax
from jax.experimental import pallas as pl
from jax.experimental.pallas import tpu as pltpu
from jax.sharding import PartitionSpec as P

MESH = pl.DeviceIdType.MESH
NT = (((1,), (1,)), ((), ()))
NN = (((1,), (0,)), ((), ()))
f32 = jnp.float32
bf16 = jnp.bfloat16


def mm(a, b, dims=NN):
    return lax.dot_general(a, b, dims, preferred_element_type=f32)


def mm_split(a, b, dims):
    high = a.astype(bf16)
    low = (a - high.astype(f32)).astype(bf16)
    return mm(high, b, dims) + mm(low, b, dims)


def level_table(leaf_count):
    layout = []
    first, count, pair = 0, leaf_count, 0
    while count >= 1:
        layout.append((first, count, pair))
        first += count
        pair += max(count // 2, 1)
        count //= 2
    return layout


def loop(count, body, unroll):
    unroll = min(unroll, count)
    while count % unroll:
        unroll -= 1

    def step(i, carry):
        parts = [body(i * unroll + u) for u in range(unroll)]
        if hasattr(parts[0], "__next__"):
            for part in parts:
                next(part)
            for part in parts:
                next(part, None)
        return carry

    if count == unroll:
        step(0, 0)
    else:
        lax.fori_loop(0, count // unroll, step, 0)


def kernel(
    roots_n,
    vec, basis_h, trans_h, coup_h, near_h,
    cs, ns, tt, ts, top_t, top_c,
    out,
    vbuf, pts, basis, trans_raw, coup_raw, near, trans_rows, trans, coup,
    cp, halo, cl, field, down, near_own, near_send, near_recv,
    roots, uc, g, top_recv, top_send,
    local_sem, vs_sem, vr_sem, hs_sem, hr_sem, ns_sem, nr_sem, rs_sem, rr_sem, ts_sem, tr_sem,
):
    n = roots_n
    leaves = basis.shape[0]
    width = basis.shape[1]
    rows = vec.shape[0]
    layout = level_table(leaves)
    pairs = leaves // 2
    slots = coup_raw.shape[0]
    nodes = trans.shape[0]
    near_slots = near.shape[1]
    top_blocks = top_c.shape[0]
    me = lax.axis_index("leaf")
    mine = lax.axis_index("rhs")
    other = 1 - mine
    has_left, has_right = me > 0, me < n - 1
    odd = lax.rem(me, 2)
    buddy = me + 1 - 2 * odd
    far = me - 1 + 2 * odd
    has_far = jnp.logical_and(far >= 0, far < n)

    def peer_of(i):
        return lax.rem(me + i, n)

    barrier = pltpu.get_barrier_semaphore()

    def greet(i, carry):
        pl.semaphore_signal(barrier, inc=1, device_id=(peer_of(i), mine), device_id_type=MESH)
        return carry

    lax.fori_loop(1, n, greet, 0)
    pl.semaphore_signal(barrier, inc=1, device_id=(me, other), device_id_type=MESH)

    local = [
        pltpu.make_async_copy(src, dst, local_sem.at[i])
        for i, (src, dst) in enumerate(
            ((vec, vbuf.at[0, 0]), (basis_h, basis), (trans_h, trans_raw), (near_h, near), (coup_h, coup_raw))
        )
    ]
    for i in (0, 1, 2):
        local[i].start()


    def vec_send(kind, half):
        source = vec
        if half == 1 and kind > 0:
            source = vbuf.at[0, 1] if kind == 1 else vbuf.at[2, 0]
        if kind == 1:
            target = (buddy, mine)
        elif kind == 2 and half == 0:
            target = (far, mine)
        else:
            target = (me, other)
        return pltpu.make_async_remote_copy(
            src_ref=source, dst_ref=vbuf.at[kind, half],
            send_sem=vs_sem.at[kind, half], recv_sem=vr_sem.at[kind, half],
            device_id=target, device_id_type=MESH,
        )

    def halo_send(place, part):
        part_pairs = pl.ds(0, pairs) if part == 0 else pl.ds(pairs, cp.shape[0] - pairs)
        return pltpu.make_async_remote_copy(
            src_ref=cp.at[part_pairs], dst_ref=halo.at[place, part_pairs],
            send_sem=hs_sem.at[place, part], recv_sem=hr_sem.at[place, part],
            device_id=(me + (1 - 2 * place), mine), device_id_type=MESH,
        )

    sends_right, sends_left = has_right, has_left
    pl.semaphore_wait(barrier, n)

    @pl.when(has_far)
    def _():
        vec_send(2, 0).start()

    vec_send(0, 1).start()
    vec_send(1, 0).start()

    local[0].wait()
    local[1].wait()
    local[4].start()

    def store_pair(pair_index, node_index, a, b):
        cp[pair_index] = jnp.concatenate([a, b], axis=1)
        cl[node_index] = a
        cl[node_index + 1] = b

    def turned(a, b):
        return jnp.concatenate([a, b], axis=0).T.astype(f32)

    def transfer_layout():
        half = width // 2
        pitch = half + 8

        def turn(m):
            trans_rows[pl.ds(m, nodes, stride=pitch), :] = turned(trans_raw[m], trans_raw[m + half])

        def split(t):
            x = trans_rows[pl.ds(pl.multiple_of(t * pitch, 8), half), :].astype(bf16)
            trans[t, :half, :] = x[:, :width]
            trans[t, half:, :] = x[:, width:]

        loop(half, turn, 8)
        whole = nodes // 16 * 16
        loop(whole, split, 16)
        for t in range(whole, nodes):
            split(t)

    per = slots // 2

    def turn_coupling(k, m):
        coup[pl.ds(k * width + m, nodes, stride=per * width + 8), :] = turned(coup_raw[k, m], coup_raw[k + per, m])

    def leaf_up(p):
        x = vbuf[0, 0, :, pl.ds(pl.multiple_of(p * 2 * width, 2 * width), 2 * width)]
        x0, x1 = x[:, :width], x[:, width:]
        c0 = mm(x0, basis[2 * p]).astype(bf16)
        c1 = mm(x1, basis[2 * p + 1]).astype(bf16)
        store_pair(p, leaves + 2 * p, c0, c1)

    loop(pairs, leaf_up, 16)
    local[3].start()

    @pl.when(sends_right)
    def _():
        halo_send(0, 0).start()

    @pl.when(sends_left)
    def _():
        halo_send(1, 0).start()

    local[2].wait()
    transfer_layout()
    local[4].wait()
    early = 4
    for height in range(1, len(layout)):
        below_first, below_count, below_pair = layout[height - 1]
        first, count, pair = layout[height]

        def lift(q):
            w = trans[pl.ds(below_first + 2 * q, 2)].reshape(2 * width, width)
            return mm(cp[below_pair + q], w).astype(bf16)

        if count > 1:
            def up(p):
                a, b = lift(2 * p), lift(2 * p + 1)
                yield
                store_pair(pair + p, 3 * first + count + 2 * p, a, b)

            loop(count // 2, up, 16)
        else:
            c = lift(0)
            cp[pair] = jnp.concatenate([c, c], axis=1)
            cl[3 * first + count] = c
        for m in range(early * (height - 1), early * height):
            turn_coupling(0, m)
    root_row = layout[-1][0]
    root_pair = layout[-1][2]
    root_term = mm(cp[root_pair][:, :width], trans[root_row])

    def fold(x):
        return jnp.concatenate([x[:rows // 2], x[rows // 2:]], axis=1)

    def unfold(x):
        return jnp.concatenate([x[:, :width], x[:, width:]], axis=0)

    roots[me] = fold(root_term)

    def root_copy(i):
        return pltpu.make_async_remote_copy(
            src_ref=roots.at[me], dst_ref=roots.at[me], send_sem=rs_sem, recv_sem=rr_sem,
            device_id=(peer_of(i), mine), device_id_type=MESH,
        )

    def all_peers(buffer, send_sem, recv_sem):
        part = buffer.at[pl.ds(0, n - 1)]
        return pltpu.make_async_remote_copy(
            src_ref=part, dst_ref=part, send_sem=send_sem, recv_sem=recv_sem,
            device_id=(peer_of(1), mine), device_id_type=MESH,
        )

    def send_roots(i, carry):
        root_copy(i).start()
        return carry

    lax.fori_loop(1, n, send_roots, 0)

    @pl.when(sends_right)
    def _():
        halo_send(0, 1).start()

    @pl.when(sends_left)
    def _():
        halo_send(1, 1).start()

    vec_send(0, 1).wait_recv()
    vec_send(1, 1).start()

    @pl.when(has_far)
    def _():
        vec_send(2, 0).wait_recv()
        vec_send(2, 1).start()

    turns_done = early * (len(layout) - 1)
    loop(width - turns_done, lambda m: turn_coupling(0, turns_done + m), 8)
    for k in range(1, per):
        loop(width, lambda m: turn_coupling(k, m), 8)

    def unpack_points(kind, half):
        place = (1, 2 - 2 * odd, 2 * odd)[kind]

        def body(p):
            x = vbuf[kind, half, :, pl.ds(pl.multiple_of(p * 2 * width, 2 * width), 2 * width)]
            pts[place * leaves + 2 * p, half * rows:(half + 1) * rows, :] = x[:, :width]
            pts[place * leaves + 2 * p + 1, half * rows:(half + 1) * rows, :] = x[:, width:]

        loop(pairs, body, 16)

    @pl.when(jnp.logical_not(has_far))
    def _():
        vbuf[2] = jnp.zeros(vbuf.shape[1:], bf16)

    @pl.when(jnp.logical_not(has_left))
    def _():
        halo[0] = jnp.zeros(halo.shape[1:], bf16)

    @pl.when(jnp.logical_not(has_right))
    def _():
        halo[1] = jnp.zeros(halo.shape[1:], bf16)

    unpack_points(0, 0)
    unpack_points(0, 1)
    vec_send(1, 0).wait_recv()
    unpack_points(1, 0)
    unpack_points(2, 0)
    vec_send(1, 1).wait_recv()
    unpack_points(1, 1)

    @pl.when(has_far)
    def _():
        vec_send(2, 1).wait_recv()

    unpack_points(2, 1)
    local[3].wait()
    leaf_base = (me - 1) * leaves

    def near_leaf(i):
        x = [pts[jnp.clip(ns[j, i] - leaf_base, 0, 3 * leaves - 1)] for j in range(near_slots)]
        blocks = [near[i, j] for j in range(near_slots)]
        return mm(jnp.concatenate(x, axis=1), jnp.concatenate(blocks, axis=1), NT)

    def near_pair(p):
        both = jnp.concatenate([near_leaf(2 * p), near_leaf(2 * p + 1)], axis=1)
        near_own[p] = both[:rows]
        near_send[p] = both[rows:].astype(bf16)

    chunks = near_recv_chunks = ns_sem.shape[0]
    chunk = pairs // chunks

    def near_copy(c):
        part = pl.ds(c * chunk, chunk)
        return pltpu.make_async_remote_copy(
            src_ref=near_send.at[part], dst_ref=near_recv.at[part],
            send_sem=ns_sem.at[c], recv_sem=nr_sem.at[c],
            device_id=(me, other), device_id_type=MESH,
        )

    for c in range(chunks - 1):
        loop(chunk, lambda p: near_pair(c * chunk + p), 4)
        near_copy(c).start()

    rest = list(range((chunks - 1) * chunk, pairs))

    def near_rest(count):
        for p in rest[:count]:
            near_pair(p)
        del rest[:count]

    all_peers(roots, rs_sem, rr_sem).wait_recv()
    half_n = n // 2
    uc[0] = jnp.zeros(uc.shape[1:], bf16)
    uc[1] = jnp.zeros(uc.shape[1:], bf16)
    loop(half_n, lambda j: uc.__setitem__(half_n + j, unfold(roots[2 * j] + roots[2 * j + 1]).astype(bf16)), 4)
    size = half_n // 2
    while size >= 2:
        def upper_up(j):
            h = size + j
            x = mm(uc[2 * h], top_t[2 * h - 2]) + mm(uc[2 * h + 1], top_t[2 * h - 1])
            yield
            uc[h] = x.astype(bf16)

        loop(size, upper_up, 8)
        near_rest(2)
        size //= 2
    terms = [mm(uc[ts[b]], top_c[b]) for b in range(top_blocks)]
    near_rest(2)

    def upper_gather(j):
        h = j + 2
        total = None
        for b in range(top_blocks):
            term = terms[b] * (tt[b] == h).astype(f32)
            total = term if total is None else total + term
        g[h] = total

    loop(n - 2, upper_gather, 16)
    size = 2
    while size < half_n:
        def upper_down(j):
            h = size + j
            w = top_t[pl.ds(2 * h - 2, 2)].reshape(2 * width, width)
            x = mm_split(g[h], w, NT)
            even = g[2 * h] + x[:, :width]
            uneven = g[2 * h + 1] + x[:, width:]
            yield
            g[2 * h] = even
            g[2 * h + 1] = uneven

        loop(size, upper_down, 8)
        near_rest(1)
        size *= 2

    near_rest(len(rest))
    near_copy(chunks - 1).start()
    loop(half_n, lambda j: top_send.__setitem__(j, fold(g[half_n + j])), 8)
    top_recv[me] = top_send[me // 2]

    def top_copy(i):
        peer = peer_of(i)
        return pltpu.make_async_remote_copy(
            src_ref=top_send.at[peer // 2], dst_ref=top_recv.at[me], send_sem=ts_sem, recv_sem=tr_sem,
            device_id=(peer, mine), device_id_type=MESH,
        )

    def send_top(i, carry):
        top_copy(i).start()
        return carry

    lax.fori_loop(1, n, send_top, 0)

    for part in range(2):
        @pl.when(has_left)
        def _():
            halo_send(0, part).wait_recv()

        @pl.when(has_right)
        def _():
            halo_send(1, part).wait_recv()

    for first, count, pair in layout:
        for place in range(2):
            base = 3 * first + 2 * place * count
            if count > 1:
                def unpack(p):
                    x = halo[place, pair + p]
                    cl[base + 2 * p] = x[:, :width]
                    cl[base + 2 * p + 1] = x[:, width:]

                loop(count // 2, unpack, 16)
            else:
                cl[base] = halo[place, pair][:, :width]

    depth = slots // 2 * width
    left_half = lax.broadcasted_iota(jnp.int32, (rows, 2 * width), 1) < width

    def node_terms(height, t):
        first, count, _ = layout[height]
        base = 3 * first - (me - 1) * count
        c = [cl[jnp.clip(base + cs[k, first + t], 0, cl.shape[0] - 1)] for k in range(slots)]
        x = jnp.concatenate(
            [jnp.concatenate(c[:per], axis=1), jnp.concatenate(c[per:], axis=1)], axis=0
        )
        w = coup[pl.ds(pl.multiple_of((first + t) * (depth + 8), 8), depth), :].astype(bf16)
        r = mm(x, w)
        return r[:rows], r[rows:]

    def pair_field(height, p):
        a0, b0 = node_terms(height, 2 * p)
        a1, b1 = node_terms(height, 2 * p + 1)
        even = a0 + pltpu.roll(b0, width, 1)
        uneven = pltpu.roll(a1, width, 1) + b1
        field[layout[height][2] + p] = jnp.where(left_half, even, uneven)

    a0, b0 = node_terms(len(layout) - 1, 0)
    root_field = (a0 + pltpu.roll(b0, width, 1))[:, :width]
    for height in range(len(layout) - 2, 0, -1):
        loop(layout[height][1] // 2, lambda p: pair_field(height, p), 16)

    share = pairs // (len(layout) + 1)
    fields_done = share * (len(layout) - 3)
    loop(pairs - fields_done, lambda p: pair_field(0, fields_done + p), 16)

    all_peers(top_recv, ts_sem, tr_sem).wait_recv()
    parent = top_recv[0]
    for i in range(1, n):
        parent = parent + top_recv[i]
    parent = unfold(parent)
    root_down = (root_field + mm_split(parent, trans[root_row], NT)).astype(bf16)

    def step_down(height, q, x):
        first, count, pair = layout[height]
        w = trans[pl.ds(first + 2 * q, 2)].reshape(2 * width, width)
        return (field[pair + q] + mm(x, w, NT)).astype(bf16)

    top_height = len(layout) - 2
    down[layout[top_height][2]] = step_down(top_height, 0, root_down)
    for height in range(top_height - 1, 0, -1):
        pair = layout[height][2]
        above = layout[height + 1][2]

        def descend(p):
            x = down[above + p]
            even = step_down(height, 2 * p, x[:, :width])
            uneven = step_down(height, 2 * p + 1, x[:, width:])
            yield
            down[pair + 2 * p] = even
            down[pair + 2 * p + 1] = uneven

        loop(layout[height][1] // 4, descend, 8)
        for p in range(share * (top_height - 1 - height), share * (top_height - height)):
            pair_field(0, p)

    for c in range(chunks):
        near_copy(c).wait_recv()
    above = layout[1][2]

    def leaf_pair(p, x):
        y = step_down(0, p, x)
        far = jnp.concatenate(
            [mm(y[:, :width], basis[2 * p], NT), mm(y[:, width:], basis[2 * p + 1], NT)], axis=1
        )
        total = far + (near_own[p] + near_recv[p].astype(f32))
        out[:, pl.ds(pl.multiple_of(p * 2 * width, 2 * width), 2 * width)] = total.astype(bf16)

    def leaf_down(p):
        x = down[above + p]
        leaf_pair(2 * p, x[:, :width])
        leaf_pair(2 * p + 1, x[:, width:])

    loop(pairs // 2, leaf_down, 8)

    vec_send(0, 1).wait_send()
    vec_send(1, 0).wait_send()
    vec_send(1, 1).wait_send()

    @pl.when(has_far)
    def _():
        vec_send(2, 0).wait_send()
        vec_send(2, 1).wait_send()

    @pl.when(sends_right)
    def _():
        halo_send(0, 0).wait_send()
        halo_send(0, 1).wait_send()

    @pl.when(sends_left)
    def _():
        halo_send(1, 0).wait_send()
        halo_send(1, 1).wait_send()

    for c in range(chunks):
        near_copy(c).wait_send()

    all_peers(roots, rs_sem, rr_sem).wait_send()
    all_peers(top_recv, ts_sem, tr_sem).wait_send()


def shards(
    vectors, leaf_basis, local_transfer, coupling, coupling_source,
    top_transfer, top_coupling, top_target, top_source, near_blocks, near_source,
):
    n = lax.axis_size("leaf")
    rows = vectors.shape[0]
    leaves, width, rank = leaf_basis.shape
    nodes = local_transfer.shape[0]
    slots = coupling.shape[1]
    pairs = leaves // 2
    pair_total = leaves
    chunks = 4
    any_spec = pl.BlockSpec(memory_space=pl.ANY)
    smem = pl.BlockSpec(memory_space=pltpu.SMEM)
    vmem = pl.BlockSpec(memory_space=pltpu.VMEM)
    dma = pltpu.SemaphoreType.DMA
    return pl.pallas_call(
        functools.partial(kernel, n),
        out_shape=jax.ShapeDtypeStruct(vectors.shape, bf16),
        in_specs=[any_spec] * 5 + [smem] * 4 + [vmem] * 2,
        out_specs=vmem,
        scratch_shapes=[
            pltpu.VMEM((3, 2) + vectors.shape, bf16),
            pltpu.VMEM((3 * leaves, 2 * rows, width), bf16),
            pltpu.VMEM(leaf_basis.shape, bf16),
            pltpu.VMEM((width, rank, nodes), bf16),
            pltpu.VMEM((slots, rank, rank, nodes), bf16),
            pltpu.VMEM(near_blocks.shape, bf16),
            pltpu.VMEM((nodes * (rank // 2 + 8), 2 * rank), f32),
            pltpu.VMEM(local_transfer.shape, bf16),
            pltpu.VMEM((nodes * (slots // 2 * rank + 8), 2 * rank), f32),
            pltpu.VMEM((pair_total, rows, 2 * rank), bf16),
            pltpu.VMEM((2, pair_total, rows, 2 * rank), bf16),
            pltpu.VMEM((3 * nodes, rows, rank), bf16),
            pltpu.VMEM((pair_total, rows, 2 * rank), f32),
            pltpu.VMEM((pair_total, rows, 2 * rank), bf16),
            pltpu.VMEM((pairs, rows, 2 * width), f32),
            pltpu.VMEM((pairs, rows, 2 * width), bf16),
            pltpu.VMEM((pairs, rows, 2 * width), bf16),
            pltpu.VMEM((n, rows // 2, 2 * rank), f32),
            pltpu.VMEM((n, rows, rank), bf16),
            pltpu.VMEM((n, rows, rank), f32),
            pltpu.VMEM((n, rows // 2, 2 * rank), f32),
            pltpu.VMEM((n // 2, rows // 2, 2 * rank), f32),
            dma((5,)),
            dma((3, 2)), dma((3, 2)),
            dma((2, 2)), dma((2, 2)),
            dma((chunks,)), dma((chunks,)),
            dma, dma, dma, dma,
        ],
        compiler_params=pltpu.CompilerParams(
            collective_id=0, has_side_effects=True, vmem_limit_bytes=56 * 1024 * 1024
        ),
    )(
        vectors, leaf_basis, local_transfer.transpose(1, 2, 0), coupling.transpose(1, 2, 3, 0), near_blocks,
        coupling_source.T, near_source.T, top_target, top_source, top_transfer, top_coupling,
    )


def solution(mesh):
    placed = (
        P("rhs", "leaf"),
        P("leaf", None, None),
        P("leaf", None, None),
        P("leaf", None, None, None),
        P("leaf", None),
        P(),
        P("leaf", None, None),
        P("leaf"),
        P("leaf"),
        P("leaf", "rhs", None, None),
        P("leaf", "rhs"),
    )
    return jax.shard_map(
        shards, mesh=mesh, in_specs=placed, out_specs=P("rhs", "leaf"), check_vma=False
    )
```
